32 devices in a mesh: groups: 2 (over x), node: 4 (over y, core), local: 4 (over z).
Axes of the slice: x: 2, y: 2, z: 4, core: 2. Of those that a mesh axis runs over, the one named last changes fastest.
Arguments:
- hidden: bfloat16 [2048, 8, 1024], P(('groups', 'node', 'local')), parts along dimension 0, may hold values from -6 to 6
- gates: float32 [2048, 8], P(('groups', 'node', 'local')), parts along dimension 0, may hold values from 0.05 to 1
- node_groups: int32 [2048, 4], P(('groups', 'node', 'local')), parts along dimension 0, may hold values from 0 to 3, as said below
- group_picks: int32 [2048, 8], P(('groups', 'node', 'local')), parts along dimension 0, may hold values from 0 to 3, as said below
- down_weight: bfloat16 [16, 1024, 3584], P(('node', 'local')), may hold values from -0.1875 to 0.1875
Outputs:
- mixed: bfloat16 [2048, 3584], P(('groups', 'node', 'local')), parts along dimension 0
The draws below stay inside these ranges and needn't reach their ends.
There are 2 independent parts, one for each index of `groups`. The reference program is written for one: setup_inputs(seed, part) draws one part's arguments, and reference() takes and returns one part's arrays. A program takes and returns all parts, laid end to end along the dimension named above; an argument that names none is the same for every part. Nothing has to cross between parts.
Inputs may be any that keep to these rules, and one draw needn't show every extreme that they name: `node_groups`: each row lists 4 different node groups. `group_picks`: the picks of one listed group of a row name different experts; at most 32 rows of one device name one expert, and in every draw every expert of some node group is named by exactly 32 rows of every device.
All inputs are finite; a program needn't handle non-finite values.
Results may differ from the reference program's by a relative error of at most 0.0085.
Values may be sent and summed in bfloat16 or wider, within the bound.
A program may use at most 128 MiB of HBM per device.

```python
import math
import jax
import jax.numpy as jnp
from jax import lax

D = 3584
FF = 1024
TOPK = 8
GROUPS = 4
ROWS_DEV = 64
ROWS = 1024
EXPERTS = 16
N_NODE = 4
N_LOCAL = 4


def route_tables(key):
    row_total = ROWS_DEV * N_NODE * N_LOCAL
    block_total = N_NODE * N_LOCAL
    node_range = jnp.arange(N_NODE, dtype=jnp.int32)
    hot_node = jax.random.randint(jax.random.fold_in(key, 11), (), 0, N_NODE, dtype=jnp.int32)
    scores = jax.random.randint(jax.random.fold_in(key, 12), (row_total, N_NODE), 0, 65536, dtype=jnp.int32) * N_NODE + node_range[None, :]
    scores = jnp.where(node_range[None, :] == hot_node, -1, scores)
    chosen = jnp.argsort(scores, axis=1)[:, :GROUPS].astype(jnp.int32)
    turn = jax.random.randint(jax.random.fold_in(key, 13), (row_total, 1), 0, GROUPS, dtype=jnp.int32)
    rotate = (jnp.arange(GROUPS, dtype=jnp.int32)[None, :] + turn) % GROUPS
    node_groups = jnp.take_along_axis(chosen, rotate, axis=1)
    first_off = jax.random.randint(jax.random.fold_in(key, 14), (block_total, N_NODE), 0, N_LOCAL, dtype=jnp.int32)
    second_off = jax.random.randint(jax.random.fold_in(key, 15), (block_total, N_NODE), 1, N_LOCAL, dtype=jnp.int32)
    row_ids = jnp.arange(row_total, dtype=jnp.int32)
    block_of = row_ids // ROWS_DEV
    inner = row_ids % ROWS_DEV
    first_tab = jnp.take_along_axis(first_off[block_of], node_groups, axis=1)
    second_tab = jnp.take_along_axis(second_off[block_of], node_groups, axis=1)
    pick_one = (inner[:, None] + first_tab) % N_LOCAL
    pick_two = (pick_one + second_tab) % N_LOCAL
    group_picks = jnp.stack([pick_one, pick_two], axis=2).reshape(row_total, TOPK).astype(jnp.int32)
    return (node_groups.astype(jnp.int32), group_picks)


def draw_node_groups(key, part):
    node_groups, group_picks = route_tables(key)
    return node_groups


def draw_group_picks(key, part):
    node_groups, group_picks = route_tables(key)
    return group_picks


def level_of(rng, extent, shards, least, largest):
    def one(dim, shards_of):
        heights = jax.random.uniform(jax.random.fold_in(jax.random.fold_in(rng, 6), dim), (shards_of,), jnp.float32, least / len(shards), largest / len(shards))
        return jnp.repeat(jnp.exp(heights), extent[dim] // shards_of).reshape((-1,) + (1,) * (len(extent) - dim - 1))

    factor_of = one(*shards[0])
    for cut in shards[1:]:
        factor_of = factor_of * one(*cut)
    return factor_of


def bell_draw(key, extent, spread, limit, pieces=(), held_as=jnp.bfloat16):
    values = jax.random.normal(key, extent, jnp.float32) * spread
    if len(pieces) > 0:
        values = level_of(key, extent, pieces, -0.22, 0.18) * values
    return jnp.clip(values, min=-limit, max=limit).astype(held_as)


def setup_inputs(seed: int = 0, part: int = 0) -> dict:
    keys = jax.random.split(jax.random.key(seed), 6)
    part_keys = jax.random.split(jax.random.fold_in(keys[5], part), 6)
    hidden = bell_draw(part_keys[0], (ROWS, TOPK, FF), 1.0, 6.0, ((0, 16),))
    gates = jnp.clip(jnp.exp(math.log(1.0) - 2.9957323 * jax.random.uniform(part_keys[1], (ROWS, TOPK), jnp.float32) ** level_of(part_keys[1], (ROWS, TOPK), ((0, 16),), -0.2, 0.2)), 0.05, 1.0)
    node_groups = draw_node_groups(jax.random.fold_in(jax.random.fold_in(keys[5], part), 71), part)
    group_picks = draw_group_picks(jax.random.fold_in(jax.random.fold_in(keys[5], part), 71), part)
    down_weight = bell_draw(keys[4], (EXPERTS, FF, D), FF ** -0.5, 0.1875, ((0, 16),))
    return {"hidden": hidden, "gates": gates, "node_groups": node_groups, "group_picks": group_picks, "down_weight": down_weight}


route_scale = 2.5
row_block = 128


def reference(hidden, gates, node_groups, group_picks, down_weight):
    row_count, pick_count, hidden_width = hidden.shape
    group_count = node_groups.shape[1]
    pair_count = pick_count // group_count
    model_width = down_weight.shape[2]
    expert_count = down_weight.shape[0]
    route_weights = (route_scale * gates / jnp.sum(gates, axis=1, keepdims=True)).astype(jnp.bfloat16)
    expert_ids = (node_groups[:, :, None] * N_LOCAL + group_picks.reshape(row_count, group_count, pair_count)).reshape(-1).astype(jnp.int32)
    total = expert_ids.shape[0]
    order = jnp.argsort(expert_ids, stable=True).astype(jnp.int32)
    counts = jnp.sum((expert_ids[:, None] == jnp.arange(expert_count, dtype=jnp.int32)[None, :]).astype(jnp.int32), axis=0)
    starts = (jnp.cumsum(counts) - counts).astype(jnp.int32)
    flat_rows = hidden.reshape(total, hidden_width)
    sorted_rows = jnp.concatenate([flat_rows[order], jnp.zeros((row_block, hidden_width), hidden.dtype)], axis=0)
    padded_order = jnp.concatenate([order, jnp.full((row_block,), total, jnp.int32)])
    outputs = jnp.zeros((total + 1, model_width), jnp.bfloat16)

    def per_expert(carry, expert_id):
        weight_e = down_weight[expert_id]
        begin_e = starts[expert_id]
        count_e = counts[expert_id]

        def per_block(block_id, acc):
            start = (begin_e + block_id * row_block).astype(jnp.int32)
            rows_in = lax.dynamic_slice_in_dim(sorted_rows, start, row_block, 0)
            index_in = lax.dynamic_slice_in_dim(padded_order, start, row_block, 0)
            live = (block_id * row_block + jnp.arange(row_block, dtype=jnp.int32)) < count_e
            index_in = jnp.where(live, index_in, total).astype(jnp.int32)
            product = jnp.dot(rows_in, weight_e, preferred_element_type=jnp.float32).astype(jnp.bfloat16)
            return acc.at[index_in].set(product)

        upper = ((count_e + row_block - 1) // row_block).astype(jnp.int32)
        carry = lax.fori_loop(jnp.int32(0), upper, per_block, carry)
        return carry, None

    outputs, _ = lax.scan(per_expert, outputs, jnp.arange(expert_count, dtype=jnp.int32))
    picked = outputs[:total].astype(jnp.float32).reshape(row_count, group_count, pair_count, model_width)
    weights_f = route_weights.astype(jnp.float32).reshape(row_count, group_count, pair_count, 1)
    group_sums = jnp.sum(weights_f * picked, axis=2).astype(jnp.bfloat16)
    return jnp.sum(group_sums.astype(jnp.float32), axis=1).astype(jnp.bfloat16)
```

```python
import functools

import jax
import jax.numpy as jnp
from jax import lax
from jax.experimental import pallas as pl
from jax.experimental.pallas import tpu as pltpu
from jax.sharding import PartitionSpec as P

route_scale = 2.5
MESH = pl.DeviceIdType.MESH
BF16 = jnp.bfloat16
F32 = jnp.float32


def expert_apply(inputs, weight_block):
    flat_rows = inputs.reshape(-1, inputs.shape[-1])
    product = jnp.dot(flat_rows, weight_block, preferred_element_type=jnp.float32)
    return product.astype(jnp.bfloat16).reshape(inputs.shape[:-1] + (weight_block.shape[1],))


def slot_positions(targets, count):
    one_hot = (targets[:, None] == jnp.arange(count, dtype=jnp.int32)[None, :]).astype(jnp.int32)
    running = jnp.cumsum(one_hot, axis=0) - 1
    return jnp.sum(running * one_hot, axis=1)


def pack_rows(hidden, node_groups, pair_picks, local_count, device_count, capacity):
    hidden_width = hidden.shape[2]
    expert_ids = (node_groups[:, :, None] * local_count + pair_picks).reshape(-1)
    slot_index = expert_ids * capacity + slot_positions(expert_ids, device_count)
    outgoing = (
        jnp.zeros((device_count * capacity, hidden_width), jnp.bfloat16)
        .at[slot_index]
        .set(hidden.reshape(-1, hidden_width))
    )
    return (slot_index, outgoing)


def combine_rows(returned, slot_index, pair_weights):
    row_count, group_count, pair_count = pair_weights.shape
    model_width = returned.shape[-1]
    picked = returned.reshape(-1, model_width)[slot_index].astype(jnp.float32)
    picked = picked.reshape(row_count, group_count, pair_count, model_width)
    group_sums = jnp.sum(pair_weights.astype(jnp.float32)[..., None] * picked, axis=2).astype(
        jnp.bfloat16
    )
    return jnp.sum(group_sums.astype(jnp.float32), axis=1).astype(jnp.bfloat16)


def sparse_plan(hidden, route_weights, node_groups, group_picks, weight_block, capacity):
    row_count, pick_count, hidden_width = hidden.shape
    group_count = node_groups.shape[1]
    pair_count = pick_count // group_count
    local_count = lax.axis_size("local")
    device_count = lax.axis_size("node") * local_count
    pair_weights = route_weights.reshape(row_count, group_count, pair_count)
    pair_picks = group_picks.reshape(row_count, group_count, pair_count)
    slot_index, outgoing = pack_rows(
        hidden, node_groups, pair_picks, local_count, device_count, capacity
    )
    arrived = lax.all_to_all(
        outgoing.reshape(device_count, capacity, hidden_width),
        ("node", "local"),
        split_axis=0,
        concat_axis=0,
        tiled=True,
    )
    returned = lax.all_to_all(
        expert_apply(arrived, weight_block),
        ("node", "local"),
        split_axis=0,
        concat_axis=0,
        tiled=True,
    )
    return combine_rows(returned, slot_index, pair_weights)


def fused_kernel(
    nodes, locals_, cap, chunk,
    ids_ref, wts_ref, hid_ref, w_hbm, out_ref,
    hot, xs, xr, mix, mixr, wv, outb, zb, pb, rb,
    w_sem, xsend, xrecv, asend, arecv, zsend, zrecv, psend, precv,
):
    half = nodes // 2
    me_n = lax.axis_index("node")
    me_l = lax.axis_index("local")
    me_y, me_c = me_n // 2, me_n % 2
    rows, width = out_ref.shape
    pairs = ids_ref.shape[1]
    picks = pairs // rows
    slots = nodes * locals_ * cap
    chunks = width // chunk

    def node_to(d):
        return ((me_y + d // 2) % half) * 2 + (me_c + d % 2) % 2

    def node_from(d):
        return ((me_y - d // 2 + half) % half) * 2 + (me_c - d % 2 + 2) % 2

    def local_to(d):
        return (me_l + d) % locals_

    barrier = pltpu.get_barrier_semaphore()
    for d in range(nodes):
        for dl in range(locals_):
            if d or dl:
                pl.semaphore_signal(
                    barrier, inc=1, device_id={"node": node_to(d), "local": local_to(dl)},
                    device_id_type=MESH,
                )

    weight_copy = pltpu.make_async_copy(w_hbm.at[0], wv, w_sem)
    weight_copy.start()

    ids = ids_ref[...]
    experts = nodes * locals_
    mine = lax.broadcasted_iota(jnp.int32, (experts, pairs), 0) == ids
    mine_f = jnp.where(mine, 1.0, 0.0)
    before = lax.broadcasted_iota(jnp.int32, (pairs, pairs), 0) < lax.broadcasted_iota(
        jnp.int32, (pairs, pairs), 1
    )
    running = jnp.dot(
        mine_f.astype(BF16), jnp.where(before, 1.0, 0.0).astype(BF16), preferred_element_type=F32
    )
    place = jnp.sum(mine_f * running, axis=0, keepdims=True).astype(jnp.int32)
    slot = ids * cap + place
    hot[...] = jnp.where(
        lax.broadcasted_iota(jnp.int32, (slots, pairs), 0) == slot, 1.0, 0.0
    ).astype(BF16)
    xs[...] = (
        jnp.dot(hot[...], hid_ref[...], preferred_element_type=F32).astype(BF16).reshape(xs.shape)
    )
    row_of = lax.broadcasted_iota(jnp.int32, (rows, pairs), 1) // picks
    spread = jnp.where(
        row_of == lax.broadcasted_iota(jnp.int32, (rows, pairs), 0), wts_ref[...], 0.0
    ).astype(BF16)
    mix_all = lax.dot_general(
        spread, hot[...], (((1,), (1,)), ((), ())), preferred_element_type=F32
    ).astype(BF16)
    span = nodes * cap
    for l in range(locals_):
        mix[l] = mix_all[:, l * span:(l + 1) * span]

    pl.semaphore_wait(barrier, nodes * locals_ - 1)

    order = list(range(nodes - 1, -1, -1))
    order = [d for d in order if d >= 2] + [d for d in order if d < 2]

    def hidden_copy(d, dl):
        n_t, l_t = node_to(d), local_to(dl)
        return pltpu.make_async_remote_copy(
            src_ref=xs.at[l_t * nodes + n_t], dst_ref=xr.at[d, me_l],
            send_sem=xsend.at[d, dl], recv_sem=xrecv.at[d, dl],
            device_id={"node": n_t, "local": l_t}, device_id_type=MESH,
        )

    def mix_copy(dl):
        l_t = local_to(dl)
        return pltpu.make_async_remote_copy(
            src_ref=mix.at[l_t], dst_ref=mixr.at[me_l],
            send_sem=asend.at[dl], recv_sem=arecv.at[dl],
            device_id={"node": me_n, "local": l_t}, device_id_type=MESH,
        )

    for d in order:
        for dl in range(locals_ - 1, -1, -1):
            if d or dl:
                hidden_copy(d, dl).start()
    for dl in range(1, locals_):
        mix_copy(dl).start()
    xr[0, me_l] = xs[me_l * nodes + me_n]
    mixr[me_l] = mix[me_l]
    weight_copy.wait()

    def return_copy(c, d):
        return pltpu.make_async_remote_copy(
            src_ref=outb.at[c, d],
            dst_ref=zb.at[c, :, pl.ds(pl.multiple_of(me_n * cap, cap), cap), :],
            send_sem=zsend.at[c, d], recv_sem=zrecv.at[c, d],
            device_id={"node": node_from(d), "local": me_l}, device_id_type=MESH,
        )

    def sum_copy(c, dl):
        l_t = local_to(dl)
        return pltpu.make_async_remote_copy(
            src_ref=pb.at[c, l_t], dst_ref=rb.at[c, me_l],
            send_sem=psend.at[c, dl], recv_sem=precv.at[c, dl],
            device_id={"node": me_n, "local": l_t}, device_id_type=MESH,
        )

    for low in list(range(2, nodes, 2)) + [0]:
        for d in (low, low + 1):
            for dl in range(locals_):
                if d or dl:
                    hidden_copy(d, dl).wait_recv()

        def apply_chunk(c, carry, low=low):
            cols = pl.ds(pl.multiple_of(c * chunk, chunk), chunk)
            x = xr[low:low + 2].reshape(2 * locals_ * cap, xr.shape[-1])
            o = jnp.dot(x, wv[:, cols], preferred_element_type=F32).astype(BF16)
            o = o.reshape(2, locals_, cap, chunk)
            for k in range(2):
                if low + k:
                    outb[c, low + k] = o[k]
                    return_copy(c, low + k).start()
                else:
                    zb[c, :, pl.ds(pl.multiple_of(me_n * cap, cap), cap), :] = o[k]
            return carry

        lax.fori_loop(0, chunks, apply_chunk, 0)

    for dl in range(1, locals_):
        mix_copy(dl).wait_recv()

    def combine_chunk(c, carry):
        for d in range(1, nodes):
            return_copy(c, d).wait_recv()
        for l in range(locals_):
            pb[c, l] = jnp.dot(mixr[l], zb[c, l], preferred_element_type=F32).astype(BF16)
        for dl in range(locals_ - 1, 0, -1):
            sum_copy(c, dl).start()
        rb[c, me_l] = pb[c, me_l]
        return carry

    lax.fori_loop(0, chunks, combine_chunk, 0)

    def final_chunk(c, carry):
        cols = pl.ds(pl.multiple_of(c * chunk, chunk), chunk)
        for dl in range(1, locals_):
            sum_copy(c, dl).wait_recv()
        total = rb[c, 0].astype(F32)
        for l in range(1, locals_):
            total = total + rb[c, l].astype(F32)
        out_ref[:, cols] = total.astype(BF16)
        return carry

    lax.fori_loop(0, chunks, final_chunk, 0)

    for d in range(nodes):
        for dl in range(locals_):
            if d or dl:
                hidden_copy(d, dl).wait_send()
    for dl in range(1, locals_):
        mix_copy(dl).wait_send()

    def drain(c, carry):
        for d in range(1, nodes):
            return_copy(c, d).wait_send()
        for dl in range(1, locals_):
            sum_copy(c, dl).wait_send()
        return carry

    lax.fori_loop(0, chunks, drain, 0)


def dense_plan(hidden, route_weights, node_groups, group_picks, down_weight, capacity):
    row_count, pick_count, hidden_width = hidden.shape
    group_count = node_groups.shape[1]
    pair_count = pick_count // group_count
    nodes = lax.axis_size("node")
    locals_ = lax.axis_size("local")
    width = down_weight.shape[2]
    pairs = row_count * pick_count
    chunk = 512 if width % 512 == 0 else 128
    chunks = width // chunk
    ids = group_picks * nodes + jnp.repeat(node_groups, pair_count, axis=1)
    dma = pltpu.SemaphoreType.DMA
    vmem = pl.BlockSpec(memory_space=pltpu.VMEM)
    return pl.pallas_call(
        functools.partial(fused_kernel, nodes, locals_, capacity, chunk),
        out_shape=jax.ShapeDtypeStruct((row_count, width), BF16),
        in_specs=[vmem, vmem, vmem, pl.BlockSpec(memory_space=pl.ANY)],
        out_specs=vmem,
        scratch_shapes=[
            pltpu.VMEM((nodes * locals_ * capacity, pairs), BF16),
            pltpu.VMEM((nodes * locals_, capacity, hidden_width), BF16),
            pltpu.VMEM((nodes, locals_, capacity, hidden_width), BF16),
            pltpu.VMEM((locals_, row_count, nodes * capacity), BF16),
            pltpu.VMEM((locals_, row_count, nodes * capacity), BF16),
            pltpu.VMEM((hidden_width, width), BF16),
            pltpu.VMEM((chunks, nodes, locals_, capacity, chunk), BF16),
            pltpu.VMEM((chunks, locals_, nodes * capacity, chunk), BF16),
            pltpu.VMEM((chunks, locals_, row_count, chunk), BF16),
            pltpu.VMEM((chunks, locals_, row_count, chunk), BF16),
            dma,
            dma((nodes, locals_)),
            dma((nodes, locals_)),
            dma((locals_,)),
            dma((locals_,)),
            dma((chunks, nodes)),
            dma((chunks, nodes)),
            dma((chunks, locals_)),
            dma((chunks, locals_)),
        ],
        compiler_params=pltpu.CompilerParams(
            collective_id=0, has_side_effects=True, vmem_limit_bytes=56 * 1024 * 1024
        ),
    )(
        ids.reshape(1, pairs),
        route_weights.astype(F32).reshape(1, pairs),
        hidden.reshape(pairs, hidden_width),
        down_weight,
    )


def shards(hidden, gates, node_groups, group_picks, down_weight):
    row_count = hidden.shape[0]
    nodes = lax.axis_size("node")
    capacity = 2 * row_count // lax.axis_size("local")
    route_weights = (route_scale * gates / jnp.sum(gates, axis=1, keepdims=True)).astype(BF16)
    if nodes == node_groups.shape[1] and nodes % 2 == 0:
        return dense_plan(hidden, route_weights, node_groups, group_picks, down_weight, capacity)
    return sparse_plan(
        hidden, route_weights, node_groups, group_picks, down_weight[0], capacity
    )


def solution(mesh):
    return jax.shard_map(
        shards,
        mesh=mesh,
        in_specs=(
            P(("groups", "node", "local"), None, None),
            P(("groups", "node", "local"), None),
            P(("groups", "node", "local"), None),
            P(("groups", "node", "local"), None),
            P(("node", "local"), None, None),
        ),
        out_specs=P(("groups", "node", "local"), None),
        check_vma=False,
    )
```

```python
import functools

import jax
import jax.numpy as jnp
from jax import lax
from jax.experimental import pallas as pl
from jax.experimental.pallas import tpu as pltpu
from jax.sharding import PartitionSpec as P

route_scale = 2.5
MESH = pl.DeviceIdType.MESH
BF16 = jnp.bfloat16
F32 = jnp.float32


def expert_apply(inputs, weight_block):
    flat_rows = inputs.reshape(-1, inputs.shape[-1])
    product = jnp.dot(flat_rows, weight_block, preferred_element_type=jnp.float32)
    return product.astype(jnp.bfloat16).reshape(inputs.shape[:-1] + (weight_block.shape[1],))


def slot_positions(targets, count):
    one_hot = (targets[:, None] == jnp.arange(count, dtype=jnp.int32)[None, :]).astype(jnp.int32)
    running = jnp.cumsum(one_hot, axis=0) - 1
    return jnp.sum(running * one_hot, axis=1)


def pack_rows(hidden, node_groups, pair_picks, local_count, device_count, capacity):
    hidden_width = hidden.shape[2]
    expert_ids = (node_groups[:, :, None] * local_count + pair_picks).reshape(-1)
    slot_index = expert_ids * capacity + slot_positions(expert_ids, device_count)
    outgoing = (
        jnp.zeros((device_count * capacity, hidden_width), jnp.bfloat16)
        .at[slot_index]
        .set(hidden.reshape(-1, hidden_width))
    )
    return (slot_index, outgoing)


def combine_rows(returned, slot_index, pair_weights):
    row_count, group_count, pair_count = pair_weights.shape
    model_width = returned.shape[-1]
    picked = returned.reshape(-1, model_width)[slot_index].astype(jnp.float32)
    picked = picked.reshape(row_count, group_count, pair_count, model_width)
    group_sums = jnp.sum(pair_weights.astype(jnp.float32)[..., None] * picked, axis=2).astype(
        jnp.bfloat16
    )
    return jnp.sum(group_sums.astype(jnp.float32), axis=1).astype(jnp.bfloat16)


def sparse_plan(hidden, route_weights, node_groups, group_picks, weight_block, capacity):
    row_count, pick_count, hidden_width = hidden.shape
    group_count = node_groups.shape[1]
    pair_count = pick_count // group_count
    local_count = lax.axis_size("local")
    device_count = lax.axis_size("node") * local_count
    pair_weights = route_weights.reshape(row_count, group_count, pair_count)
    pair_picks = group_picks.reshape(row_count, group_count, pair_count)
    slot_index, outgoing = pack_rows(
        hidden, node_groups, pair_picks, local_count, device_count, capacity
    )
    arrived = lax.all_to_all(
        outgoing.reshape(device_count, capacity, hidden_width),
        ("node", "local"),
        split_axis=0,
        concat_axis=0,
        tiled=True,
    )
    returned = lax.all_to_all(
        expert_apply(arrived, weight_block),
        ("node", "local"),
        split_axis=0,
        concat_axis=0,
        tiled=True,
    )
    return combine_rows(returned, slot_index, pair_weights)


def fused_kernel(
    nodes, locals_, cap, chunk,
    ids_ref, wts_ref, hid_ref, w_hbm, out_ref,
    hot, xs, xr, mix, mixr, wv, outb, zb, pb, mb, rb,
    w_sem, xsend, xrecv, asend, arecv, zsend, zrecv, psend, precv,
):
    half = nodes // 2
    me_n = lax.axis_index("node")
    me_l = lax.axis_index("local")
    me_y, me_c = me_n // 2, me_n % 2
    rows, width = out_ref.shape
    pairs = ids_ref.shape[1]
    picks = pairs // rows
    slots = nodes * locals_ * cap
    chunks = width // chunk

    def node_to(d):
        return ((me_y + d // 2) % half) * 2 + (me_c + d % 2) % 2

    def node_from(d):
        return ((me_y - d // 2 + half) % half) * 2 + (me_c - d % 2 + 2) % 2

    def local_to(d):
        return (me_l + d) % locals_

    barrier = pltpu.get_barrier_semaphore()
    for d in range(nodes):
        for dl in range(locals_):
            if d or dl:
                pl.semaphore_signal(
                    barrier, inc=1, device_id={"node": node_to(d), "local": local_to(dl)},
                    device_id_type=MESH,
                )

    weight_copy = pltpu.make_async_copy(w_hbm.at[0], wv, w_sem)
    weight_copy.start()

    ids = ids_ref[...]
    experts = nodes * locals_
    mine = lax.broadcasted_iota(jnp.int32, (experts, pairs), 0) == ids
    mine_f = jnp.where(mine, 1.0, 0.0)
    before = lax.broadcasted_iota(jnp.int32, (pairs, pairs), 0) < lax.broadcasted_iota(
        jnp.int32, (pairs, pairs), 1
    )
    running = jnp.dot(
        mine_f.astype(BF16), jnp.where(before, 1.0, 0.0).astype(BF16), preferred_element_type=F32
    )
    place = jnp.sum(mine_f * running, axis=0, keepdims=True).astype(jnp.int32)
    slot = ids * cap + place
    hot[...] = jnp.where(
        lax.broadcasted_iota(jnp.int32, (slots, pairs), 0) == slot, 1.0, 0.0
    ).astype(BF16)
    xs[...] = (
        jnp.dot(hot[...], hid_ref[...], preferred_element_type=F32).astype(BF16).reshape(xs.shape)
    )
    row_of = lax.broadcasted_iota(jnp.int32, (rows, pairs), 1) // picks
    spread = jnp.where(
        row_of == lax.broadcasted_iota(jnp.int32, (rows, pairs), 0), wts_ref[...], 0.0
    ).astype(BF16)
    mix_all = lax.dot_general(
        spread, hot[...], (((1,), (1,)), ((), ())), preferred_element_type=F32
    ).astype(BF16)
    span = nodes * cap
    for l in range(locals_):
        mix[l] = mix_all[:, l * span:(l + 1) * span]

    pl.semaphore_wait(barrier, nodes * locals_ - 1)

    order = list(range(nodes - 1, -1, -1))
    order = [d for d in order if d >= 2] + [d for d in order if d < 2]

    def hidden_copy(d, dl):
        n_t, l_t = node_to(d), local_to(dl)
        return pltpu.make_async_remote_copy(
            src_ref=xs.at[l_t * nodes + n_t], dst_ref=xr.at[d, me_l],
            send_sem=xsend.at[d, dl], recv_sem=xrecv.at[d, dl],
            device_id={"node": n_t, "local": l_t}, device_id_type=MESH,
        )

    def mix_copy(dl):
        l_t = local_to(dl)
        return pltpu.make_async_remote_copy(
            src_ref=mix.at[l_t], dst_ref=mixr.at[me_l],
            send_sem=asend.at[dl], recv_sem=arecv.at[dl],
            device_id={"node": me_n, "local": l_t}, device_id_type=MESH,
        )

    for d in order:
        for dl in range(locals_ - 1, -1, -1):
            if d or dl:
                hidden_copy(d, dl).start()
    for dl in range(1, locals_):
        mix_copy(dl).start()
    xr[0, me_l] = xs[me_l * nodes + me_n]
    mixr[me_l] = mix[me_l]
    weight_copy.wait()

    def return_copy(c, d):
        return pltpu.make_async_remote_copy(
            src_ref=outb.at[c, d],
            dst_ref=zb.at[c, :, pl.ds(pl.multiple_of(me_n * cap, cap), cap), :],
            send_sem=zsend.at[c, d], recv_sem=zrecv.at[c, d],
            device_id={"node": node_from(d), "local": me_l}, device_id_type=MESH,
        )

    side = me_l // 2
    mate = me_l + 1 - 2 * (me_l % 2)
    inner = me_l == 1 + side
    edge = me_l != 1 + side
    away = (1 - side) * 2

    def mate_copy(c):
        return pltpu.make_async_remote_copy(
            src_ref=pb.at[c, mate], dst_ref=rb.at[c, 0],
            send_sem=psend.at[c, 0], recv_sem=precv.at[c, 0],
            device_id={"node": me_n, "local": mate}, device_id_type=MESH,
        )

    def forward_copy(c):
        return pltpu.make_async_remote_copy(
            src_ref=pb.at[c, pl.ds(away, 2)], dst_ref=mb.at[c],
            send_sem=psend.at[c, 1], recv_sem=precv.at[c, 1],
            device_id={"node": me_n, "local": mate}, device_id_type=MESH,
        )

    def cross_copy(c, t):
        return pltpu.make_async_remote_copy(
            src_ref=mb.at[c, t], dst_ref=rb.at[c, 1],
            send_sem=psend.at[c, 2 + t], recv_sem=precv.at[c, 2],
            device_id={"node": me_n, "local": away + t}, device_id_type=MESH,
        )

    for low in list(range(2, nodes, 2)) + [0]:
        for d in (low, low + 1):
            for dl in range(locals_):
                if d or dl:
                    hidden_copy(d, dl).wait_recv()

        def apply_chunk(c, carry, low=low):
            cols = pl.ds(pl.multiple_of(c * chunk, chunk), chunk)
            x = xr[low:low + 2].reshape(2 * locals_ * cap, xr.shape[-1])
            o = jnp.dot(x, wv[:, cols], preferred_element_type=F32).astype(BF16)
            o = o.reshape(2, locals_, cap, chunk)
            for k in range(2):
                if low + k:
                    outb[c, low + k] = o[k]
                    return_copy(c, low + k).start()
                else:
                    zb[c, :, pl.ds(pl.multiple_of(me_n * cap, cap), cap), :] = o[k]
            return carry

        lax.fori_loop(0, chunks, apply_chunk, 0)

    for dl in range(1, locals_):
        mix_copy(dl).wait_recv()

    def combine(c):
        for d in range(1, nodes):
            return_copy(c, d).wait_recv()
        for l in range(locals_):
            pb[c, l] = jnp.dot(mixr[l], zb[c, l], preferred_element_type=F32).astype(BF16)

        @pl.when(edge)
        def _():
            forward_copy(c).start()

        mate_copy(c).start()

    def merge(c):
        @pl.when(inner)
        def _():
            forward_copy(c).wait_recv()
            for t in range(2):
                mb[c, t] = (mb[c, t].astype(F32) + pb[c, away + t].astype(F32)).astype(BF16)
                cross_copy(c, t).start()

    def combine_chunk(c, carry):
        combine(c)
        merge(c - 1)
        return carry

    combine(0)
    lax.fori_loop(1, chunks, combine_chunk, 0)
    merge(chunks - 1)

    def final_chunk(c, carry):
        cols = pl.ds(pl.multiple_of(c * chunk, chunk), chunk)
        mate_copy(c).wait_recv()
        cross_copy(c, 0).wait_recv()
        total = pb[c, me_l].astype(F32) + rb[c, 0].astype(F32) + rb[c, 1].astype(F32)
        out_ref[:, cols] = total.astype(BF16)
        return carry

    lax.fori_loop(0, chunks, final_chunk, 0)

    for d in range(nodes):
        for dl in range(locals_):
            if d or dl:
                hidden_copy(d, dl).wait_send()
    for dl in range(1, locals_):
        mix_copy(dl).wait_send()

    def drain(c, carry):
        for d in range(1, nodes):
            return_copy(c, d).wait_send()
        mate_copy(c).wait_send()

        @pl.when(edge)
        def _():
            forward_copy(c).wait_send()

        @pl.when(inner)
        def _():
            for t in range(2):
                cross_copy(c, t).wait_send()

        return carry

    lax.fori_loop(0, chunks, drain, 0)


def dense_plan(hidden, route_weights, node_groups, group_picks, down_weight, capacity):
    row_count, pick_count, hidden_width = hidden.shape
    group_count = node_groups.shape[1]
    pair_count = pick_count // group_count
    nodes = lax.axis_size("node")
    locals_ = lax.axis_size("local")
    width = down_weight.shape[2]
    pairs = row_count * pick_count
    chunk = 512 if width % 512 == 0 else 128
    chunks = width // chunk
    ids = group_picks * nodes + jnp.repeat(node_groups, pair_count, axis=1)
    dma = pltpu.SemaphoreType.DMA
    vmem = pl.BlockSpec(memory_space=pltpu.VMEM)
    return pl.pallas_call(
        functools.partial(fused_kernel, nodes, locals_, capacity, chunk),
        out_shape=jax.ShapeDtypeStruct((row_count, width), BF16),
        in_specs=[vmem, vmem, vmem, pl.BlockSpec(memory_space=pl.ANY)],
        out_specs=vmem,
        scratch_shapes=[
            pltpu.VMEM((nodes * locals_ * capacity, pairs), BF16),
            pltpu.VMEM((nodes * locals_, capacity, hidden_width), BF16),
            pltpu.VMEM((nodes, locals_, capacity, hidden_width), BF16),
            pltpu.VMEM((locals_, row_count, nodes * capacity), BF16),
            pltpu.VMEM((locals_, row_count, nodes * capacity), BF16),
            pltpu.VMEM((hidden_width, width), BF16),
            pltpu.VMEM((chunks, nodes, locals_, capacity, chunk), BF16),
            pltpu.VMEM((chunks, locals_, nodes * capacity, chunk), BF16),
            pltpu.VMEM((chunks, locals_, row_count, chunk), BF16),
            pltpu.VMEM((chunks, 2, row_count, chunk), BF16),
            pltpu.VMEM((chunks, 2, row_count, chunk), BF16),
            dma,
            dma((nodes, locals_)),
            dma((nodes, locals_)),
            dma((locals_,)),
            dma((locals_,)),
            dma((chunks, nodes)),
            dma((chunks, nodes)),
            dma((chunks, 4)),
            dma((chunks, 3)),
        ],
        compiler_params=pltpu.CompilerParams(
            collective_id=0, has_side_effects=True, vmem_limit_bytes=56 * 1024 * 1024
        ),
    )(
        ids.reshape(1, pairs),
        route_weights.astype(F32).reshape(1, pairs),
        hidden.reshape(pairs, hidden_width),
        down_weight,
    )


def shards(hidden, gates, node_groups, group_picks, down_weight):
    row_count = hidden.shape[0]
    nodes = lax.axis_size("node")
    capacity = 2 * row_count // lax.axis_size("local")
    route_weights = (route_scale * gates / jnp.sum(gates, axis=1, keepdims=True)).astype(BF16)
    if nodes == node_groups.shape[1] and nodes % 2 == 0 and lax.axis_size("local") == 4:
        return dense_plan(hidden, route_weights, node_groups, group_picks, down_weight, capacity)
    return sparse_plan(
        hidden, route_weights, node_groups, group_picks, down_weight[0], capacity
    )


def solution(mesh):
    return jax.shard_map(
        shards,
        mesh=mesh,
        in_specs=(
            P(("groups", "node", "local"), None, None),
            P(("groups", "node", "local"), None),
            P(("groups", "node", "local"), None),
            P(("groups", "node", "local"), None),
            P(("node", "local"), None, None),
        ),
        out_specs=P(("groups", "node", "local"), None),
        check_vma=False,
    )
```

```python
import functools

import jax
import jax.numpy as jnp
from jax import lax
from jax.experimental import pallas as pl
from jax.experimental.pallas import tpu as pltpu
from jax.sharding import PartitionSpec as P

route_scale = 2.5
MESH = pl.DeviceIdType.MESH
BF16 = jnp.bfloat16
F32 = jnp.float32


def expert_apply(inputs, weight_block):
    flat_rows = inputs.reshape(-1, inputs.shape[-1])
    product = jnp.dot(flat_rows, weight_block, preferred_element_type=jnp.float32)
    return product.astype(jnp.bfloat16).reshape(inputs.shape[:-1] + (weight_block.shape[1],))


def slot_positions(targets, count):
    one_hot = (targets[:, None] == jnp.arange(count, dtype=jnp.int32)[None, :]).astype(jnp.int32)
    running = jnp.cumsum(one_hot, axis=0) - 1
    return jnp.sum(running * one_hot, axis=1)


def pack_rows(hidden, node_groups, pair_picks, local_count, device_count, capacity):
    hidden_width = hidden.shape[2]
    expert_ids = (node_groups[:, :, None] * local_count + pair_picks).reshape(-1)
    slot_index = expert_ids * capacity + slot_positions(expert_ids, device_count)
    outgoing = (
        jnp.zeros((device_count * capacity, hidden_width), jnp.bfloat16)
        .at[slot_index]
        .set(hidden.reshape(-1, hidden_width))
    )
    return (slot_index, outgoing)


def combine_rows(returned, slot_index, pair_weights):
    row_count, group_count, pair_count = pair_weights.shape
    model_width = returned.shape[-1]
    picked = returned.reshape(-1, model_width)[slot_index].astype(jnp.float32)
    picked = picked.reshape(row_count, group_count, pair_count, model_width)
    group_sums = jnp.sum(pair_weights.astype(jnp.float32)[..., None] * picked, axis=2).astype(
        jnp.bfloat16
    )
    return jnp.sum(group_sums.astype(jnp.float32), axis=1).astype(jnp.bfloat16)


def sparse_plan(hidden, route_weights, node_groups, group_picks, weight_block, capacity):
    row_count, pick_count, hidden_width = hidden.shape
    group_count = node_groups.shape[1]
    pair_count = pick_count // group_count
    local_count = lax.axis_size("local")
    device_count = lax.axis_size("node") * local_count
    pair_weights = route_weights.reshape(row_count, group_count, pair_count)
    pair_picks = group_picks.reshape(row_count, group_count, pair_count)
    slot_index, outgoing = pack_rows(
        hidden, node_groups, pair_picks, local_count, device_count, capacity
    )
    arrived = lax.all_to_all(
        outgoing.reshape(device_count, capacity, hidden_width),
        ("node", "local"),
        split_axis=0,
        concat_axis=0,
        tiled=True,
    )
    returned = lax.all_to_all(
        expert_apply(arrived, weight_block),
        ("node", "local"),
        split_axis=0,
        concat_axis=0,
        tiled=True,
    )
    return combine_rows(returned, slot_index, pair_weights)


def fused_kernel(
    nodes, locals_, cap, chunk,
    ids_ref, wts_ref, hid_ref, w_hbm, out_ref,
    hot, xs, xr, mix, mixr, wv, outb, zb, pb, mb, rb,
    w_sem, xsend, xrecv, asend, arecv, zsend, zrecv, psend, precv,
):
    half = nodes // 2
    me_n = lax.axis_index("node")
    me_l = lax.axis_index("local")
    me_y, me_c = me_n // 2, me_n % 2
    rows, width = out_ref.shape
    pairs = ids_ref.shape[1]
    picks = pairs // rows
    slots = nodes * locals_ * cap
    chunks = width // chunk

    def node_to(d):
        return ((me_y + d // 2) % half) * 2 + (me_c + d % 2) % 2

    def node_from(d):
        return ((me_y - d // 2 + half) % half) * 2 + (me_c - d % 2 + 2) % 2

    def local_to(d):
        return (me_l + d) % locals_

    barrier = pltpu.get_barrier_semaphore()
    for d in range(nodes):
        for dl in range(locals_):
            if d or dl:
                pl.semaphore_signal(
                    barrier, inc=1, device_id={"node": node_to(d), "local": local_to(dl)},
                    device_id_type=MESH,
                )

    weight_copy = pltpu.make_async_copy(w_hbm.at[0], wv, w_sem)
    weight_copy.start()

    ids = ids_ref[...]
    experts = nodes * locals_
    mine = lax.broadcasted_iota(jnp.int32, (experts, pairs), 0) == ids
    mine_f = jnp.where(mine, 1.0, 0.0)
    before = lax.broadcasted_iota(jnp.int32, (pairs, pairs), 0) < lax.broadcasted_iota(
        jnp.int32, (pairs, pairs), 1
    )
    running = jnp.dot(
        mine_f.astype(BF16), jnp.where(before, 1.0, 0.0).astype(BF16), preferred_element_type=F32
    )
    place = jnp.sum(mine_f * running, axis=0, keepdims=True).astype(jnp.int32)
    slot = ids * cap + place
    hot[...] = jnp.where(
        lax.broadcasted_iota(jnp.int32, (slots, pairs), 0) == slot, 1.0, 0.0
    ).astype(BF16)
    xs[...] = (
        jnp.dot(hot[...], hid_ref[...], preferred_element_type=F32).astype(BF16).reshape(xs.shape)
    )
    row_of = lax.broadcasted_iota(jnp.int32, (rows, pairs), 1) // picks
    spread = jnp.where(
        row_of == lax.broadcasted_iota(jnp.int32, (rows, pairs), 0), wts_ref[...], 0.0
    ).astype(BF16)
    mix_all = lax.dot_general(
        spread, hot[...], (((1,), (1,)), ((), ())), preferred_element_type=F32
    ).astype(BF16)
    span = nodes * cap
    for l in range(locals_):
        mix[l] = mix_all[:, l * span:(l + 1) * span]

    pl.semaphore_wait(barrier, nodes * locals_ - 1)

    side = me_l // 2
    mate = me_l + 1 - 2 * (me_l % 2)
    inner = me_l == 1 + side
    edge = me_l != 1 + side
    away = (1 - side) * 2

    def place_of(q):
        return (me_l, mate, away, away + 1)[q]

    def hidden_copy(d, q):
        n_t, l_t = node_to(d), place_of(q)
        return pltpu.make_async_remote_copy(
            src_ref=xs.at[l_t * nodes + n_t], dst_ref=xr.at[d, me_l],
            send_sem=xsend.at[d, q], recv_sem=xrecv.at[d, me_l],
            device_id={"node": n_t, "local": l_t}, device_id_type=MESH,
        )

    def hidden_wait(d, l):
        pltpu.make_async_remote_copy(
            src_ref=xs.at[0], dst_ref=xr.at[d, l],
            send_sem=xsend.at[d, 0], recv_sem=xrecv.at[d, l],
            device_id={"node": me_n, "local": me_l}, device_id_type=MESH,
        ).wait_recv()

    def mix_copy(dl):
        l_t = local_to(dl)
        return pltpu.make_async_remote_copy(
            src_ref=mix.at[l_t], dst_ref=mixr.at[me_l],
            send_sem=asend.at[dl], recv_sem=arecv.at[dl],
            device_id={"node": me_n, "local": l_t}, device_id_type=MESH,
        )

    cross_nodes = list(range(2, nodes))
    for ds, qs in ((cross_nodes, (0, 1)), (cross_nodes, (2, 3)), ((1, 0), (2, 3, 1, 0))):
        for q in qs:
            for d in ds:
                if d or q:
                    hidden_copy(d, q).start()
    for dl in range(1, locals_):
        mix_copy(dl).start()
    xr[0, me_l] = xs[me_l * nodes + me_n]
    mixr[me_l] = mix[me_l]
    weight_copy.wait()

    def half_of(h):
        return pl.ds(side * 2 if h == 0 else away, 2)

    my_slots = pl.ds(pl.multiple_of(me_n * cap, cap), cap)

    def return_copy(c, d, h):
        return pltpu.make_async_remote_copy(
            src_ref=outb.at[c, d, half_of(h)],
            dst_ref=zb.at[c, half_of(h), my_slots, :],
            send_sem=zsend.at[c, d, h], recv_sem=zrecv.at[c, d, h],
            device_id={"node": node_from(d), "local": me_l}, device_id_type=MESH,
        )

    def mate_copy(c):
        return pltpu.make_async_remote_copy(
            src_ref=pb.at[c, mate], dst_ref=rb.at[c, 0],
            send_sem=psend.at[c, 0], recv_sem=precv.at[c, 0],
            device_id={"node": me_n, "local": mate}, device_id_type=MESH,
        )

    def forward_copy(c):
        return pltpu.make_async_remote_copy(
            src_ref=pb.at[c, pl.ds(away, 2)], dst_ref=mb.at[c],
            send_sem=psend.at[c, 1], recv_sem=precv.at[c, 1],
            device_id={"node": me_n, "local": mate}, device_id_type=MESH,
        )

    def cross_copy(c, t):
        return pltpu.make_async_remote_copy(
            src_ref=mb.at[c, t], dst_ref=rb.at[c, 1],
            send_sem=psend.at[c, 2 + t], recv_sem=precv.at[c, 2],
            device_id={"node": me_n, "local": away + t}, device_id_type=MESH,
        )

    for h in range(2):
        for d in cross_nodes:
            for t in range(2):
                hidden_wait(d, half_of(h).start + t)

        def cross_chunk(c, carry, h=h):
            cols = pl.ds(pl.multiple_of(c * chunk, chunk), chunk)
            x = xr[2:nodes, half_of(h)].reshape((nodes - 2) * 2 * cap, xr.shape[-1])
            o = jnp.dot(x, wv[:, cols], preferred_element_type=F32).astype(BF16)
            o = o.reshape(nodes - 2, 2, cap, chunk)
            for d in cross_nodes:
                outb[c, d, half_of(h)] = o[d - 2]
                return_copy(c, d, h).start()
            return carry

        lax.fori_loop(0, chunks, cross_chunk, 0)

    for q in range(4):
        hidden_wait(1, place_of(q))
        if q:
            hidden_wait(0, place_of(q))

    def near_chunk(c, carry):
        cols = pl.ds(pl.multiple_of(c * chunk, chunk), chunk)
        x = xr[0:2].reshape(2 * locals_ * cap, xr.shape[-1])
        o = jnp.dot(x, wv[:, cols], preferred_element_type=F32).astype(BF16)
        o = o.reshape(2, locals_, cap, chunk)
        outb[c, 1] = o[1]
        for h in range(2):
            return_copy(c, 1, h).start()
        zb[c, :, my_slots, :] = o[0]
        return carry

    lax.fori_loop(0, chunks, near_chunk, 0)

    for dl in range(1, locals_):
        mix_copy(dl).wait_recv()

    def combine(c, h):
        for d in range(1, nodes):
            return_copy(c, d, h).wait_recv()
        for t in range(2):
            l = half_of(h).start + t
            pb[c, l] = jnp.dot(mixr[l], zb[c, l], preferred_element_type=F32).astype(BF16)

    def combine_own(c, carry):
        combine(c, 0)
        mate_copy(c).start()
        return carry

    def combine_away(c):
        combine(c, 1)

        @pl.when(edge)
        def _():
            forward_copy(c).start()

    def merge(c):
        @pl.when(inner)
        def _():
            forward_copy(c).wait_recv()
            for t in range(2):
                mb[c, t] = (mb[c, t].astype(F32) + pb[c, away + t].astype(F32)).astype(BF16)
                cross_copy(c, t).start()

    def combine_chunk(c, carry):
        combine_away(c)
        merge(c - 1)
        return carry

    lax.fori_loop(0, chunks, combine_own, 0)
    combine_away(0)
    lax.fori_loop(1, chunks, combine_chunk, 0)
    merge(chunks - 1)

    def final_chunk(c, carry):
        cols = pl.ds(pl.multiple_of(c * chunk, chunk), chunk)
        mate_copy(c).wait_recv()
        cross_copy(c, 0).wait_recv()
        total = pb[c, me_l].astype(F32) + rb[c, 0].astype(F32) + rb[c, 1].astype(F32)
        out_ref[:, cols] = total.astype(BF16)
        return carry

    lax.fori_loop(0, chunks, final_chunk, 0)

    for d in range(nodes):
        for q in range(4):
            if d or q:
                hidden_copy(d, q).wait_send()
    for dl in range(1, locals_):
        mix_copy(dl).wait_send()

    def drain(c, carry):
        for d in range(1, nodes):
            for h in range(2):
                return_copy(c, d, h).wait_send()
        mate_copy(c).wait_send()

        @pl.when(edge)
        def _():
            forward_copy(c).wait_send()

        @pl.when(inner)
        def _():
            for t in range(2):
                cross_copy(c, t).wait_send()

        return carry

    lax.fori_loop(0, chunks, drain, 0)


def dense_plan(hidden, route_weights, node_groups, group_picks, down_weight, capacity):
    row_count, pick_count, hidden_width = hidden.shape
    group_count = node_groups.shape[1]
    pair_count = pick_count // group_count
    nodes = lax.axis_size("node")
    locals_ = lax.axis_size("local")
    width = down_weight.shape[2]
    pairs = row_count * pick_count
    chunk = 512 if width % 512 == 0 else 128
    chunks = width // chunk
    ids = group_picks * nodes + jnp.repeat(node_groups, pair_count, axis=1)
    dma = pltpu.SemaphoreType.DMA
    vmem = pl.BlockSpec(memory_space=pltpu.VMEM)
    return pl.pallas_call(
        functools.partial(fused_kernel, nodes, locals_, capacity, chunk),
        out_shape=jax.ShapeDtypeStruct((row_count, width), BF16),
        in_specs=[vmem, vmem, vmem, pl.BlockSpec(memory_space=pl.ANY)],
        out_specs=vmem,
        scratch_shapes=[
            pltpu.VMEM((nodes * locals_ * capacity, pairs), BF16),
            pltpu.VMEM((nodes * locals_, capacity, hidden_width), BF16),
            pltpu.VMEM((nodes, locals_, capacity, hidden_width), BF16),
            pltpu.VMEM((locals_, row_count, nodes * capacity), BF16),
            pltpu.VMEM((locals_, row_count, nodes * capacity), BF16),
            pltpu.VMEM((hidden_width, width), BF16),
            pltpu.VMEM((chunks, nodes, locals_, capacity, chunk), BF16),
            pltpu.VMEM((chunks, locals_, nodes * capacity, chunk), BF16),
            pltpu.VMEM((chunks, locals_, row_count, chunk), BF16),
            pltpu.VMEM((chunks, 2, row_count, chunk), BF16),
            pltpu.VMEM((chunks, 2, row_count, chunk), BF16),
            dma,
            dma((nodes, locals_)),
            dma((nodes, locals_)),
            dma((locals_,)),
            dma((locals_,)),
            dma((chunks, nodes, 2)),
            dma((chunks, nodes, 2)),
            dma((chunks, 4)),
            dma((chunks, 3)),
        ],
        compiler_params=pltpu.CompilerParams(
            collective_id=0, has_side_effects=True, vmem_limit_bytes=56 * 1024 * 1024
        ),
    )(
        ids.reshape(1, pairs),
        route_weights.astype(F32).reshape(1, pairs),
        hidden.reshape(pairs, hidden_width),
        down_weight,
    )


def shards(hidden, gates, node_groups, group_picks, down_weight):
    row_count = hidden.shape[0]
    nodes = lax.axis_size("node")
    capacity = 2 * row_count // lax.axis_size("local")
    route_weights = (route_scale * gates / jnp.sum(gates, axis=1, keepdims=True)).astype(BF16)
    if nodes == node_groups.shape[1] and nodes % 2 == 0 and lax.axis_size("local") == 4:
        return dense_plan(hidden, route_weights, node_groups, group_picks, down_weight, capacity)
    return sparse_plan(
        hidden, route_weights, node_groups, group_picks, down_weight[0], capacity
    )


def solution(mesh):
    return jax.shard_map(
        shards,
        mesh=mesh,
        in_specs=(
            P(("groups", "node", "local"), None, None),
            P(("groups", "node", "local"), None),
            P(("groups", "node", "local"), None),
            P(("groups", "node", "local"), None),
            P(("node", "local"), None, None),
        ),
        out_specs=P(("groups", "node", "local"), None),
        check_vma=False,
    )
```

```python
import functools

import jax
import jax.numpy as jnp
from jax import lax
from jax.experimental import pallas as pl
from jax.experimental.pallas import tpu as pltpu
from jax.sharding import PartitionSpec as P

route_scale = 2.5
MESH = pl.DeviceIdType.MESH
BF16 = jnp.bfloat16
F32 = jnp.float32


def expert_apply(inputs, weight_block):
    flat_rows = inputs.reshape(-1, inputs.shape[-1])
    product = jnp.dot(flat_rows, weight_block, preferred_element_type=jnp.float32)
    return product.astype(jnp.bfloat16).reshape(inputs.shape[:-1] + (weight_block.shape[1],))


def slot_positions(targets, count):
    one_hot = (targets[:, None] == jnp.arange(count, dtype=jnp.int32)[None, :]).astype(jnp.int32)
    running = jnp.cumsum(one_hot, axis=0) - 1
    return jnp.sum(running * one_hot, axis=1)


def pack_rows(hidden, node_groups, pair_picks, local_count, device_count, capacity):
    hidden_width = hidden.shape[2]
    expert_ids = (node_groups[:, :, None] * local_count + pair_picks).reshape(-1)
    slot_index = expert_ids * capacity + slot_positions(expert_ids, device_count)
    outgoing = (
        jnp.zeros((device_count * capacity, hidden_width), jnp.bfloat16)
        .at[slot_index]
        .set(hidden.reshape(-1, hidden_width))
    )
    return (slot_index, outgoing)


def combine_rows(returned, slot_index, pair_weights):
    row_count, group_count, pair_count = pair_weights.shape
    model_width = returned.shape[-1]
    picked = returned.reshape(-1, model_width)[slot_index].astype(jnp.float32)
    picked = picked.reshape(row_count, group_count, pair_count, model_width)
    group_sums = jnp.sum(pair_weights.astype(jnp.float32)[..., None] * picked, axis=2).astype(
        jnp.bfloat16
    )
    return jnp.sum(group_sums.astype(jnp.float32), axis=1).astype(jnp.bfloat16)


def sparse_plan(hidden, route_weights, node_groups, group_picks, weight_block, capacity):
    row_count, pick_count, hidden_width = hidden.shape
    group_count = node_groups.shape[1]
    pair_count = pick_count // group_count
    local_count = lax.axis_size("local")
    device_count = lax.axis_size("node") * local_count
    pair_weights = route_weights.reshape(row_count, group_count, pair_count)
    pair_picks = group_picks.reshape(row_count, group_count, pair_count)
    slot_index, outgoing = pack_rows(
        hidden, node_groups, pair_picks, local_count, device_count, capacity
    )
    arrived = lax.all_to_all(
        outgoing.reshape(device_count, capacity, hidden_width),
        ("node", "local"),
        split_axis=0,
        concat_axis=0,
        tiled=True,
    )
    returned = lax.all_to_all(
        expert_apply(arrived, weight_block),
        ("node", "local"),
        split_axis=0,
        concat_axis=0,
        tiled=True,
    )
    return combine_rows(returned, slot_index, pair_weights)


def fused_kernel(
    nodes, locals_, cap, chunk,
    gates_ref, groups_ref, picks_ref, hid_ref, w_hbm, out_ref,
    hot, xs, xr, mix, mixr, wv, outb, zb, pb, mb, rb,
    w_sem, xsend, xrecv, asend, arecv, zsend, zrecv, psend, precv,
):
    half = nodes // 2
    me_n = lax.axis_index("node")
    me_l = lax.axis_index("local")
    me_y, me_c = me_n // 2, me_n % 2
    rows, width = out_ref.shape
    picks, pairs = gates_ref.shape[0], hid_ref.shape[0]
    share = picks // groups_ref.shape[0]
    slots = nodes * locals_ * cap
    chunks = width // chunk

    def node_to(d):
        return ((me_y + d // 2) % half) * 2 + (me_c + d % 2) % 2

    def node_from(d):
        return ((me_y - d // 2 + half) % half) * 2 + (me_c - d % 2 + 2) % 2

    def local_to(d):
        return (me_l + d) % locals_

    barrier = pltpu.get_barrier_semaphore()
    for d in range(nodes):
        for dl in range(locals_):
            if d or dl:
                pl.semaphore_signal(
                    barrier, inc=1, device_id={"node": node_to(d), "local": local_to(dl)},
                    device_id_type=MESH,
                )

    weight_copy = pltpu.make_async_copy(w_hbm.at[0], wv, w_sem)
    weight_copy.start()

    gates = gates_ref[...]
    weights = route_scale * gates / jnp.sum(gates, axis=0, keepdims=True)
    groups = jnp.concatenate(
        [groups_ref[j // share:j // share + 1, :] for j in range(picks)], axis=0
    )
    numbers = (picks_ref[...] * nodes + groups).astype(F32)
    lay = lax.broadcasted_iota(jnp.int32, (rows, pairs), 1) // picks == lax.broadcasted_iota(
        jnp.int32, (rows, pairs), 0
    )
    tables = jnp.dot(
        jnp.concatenate([weights, numbers], axis=0).astype(BF16),
        jnp.where(lay, 1.0, 0.0).astype(BF16),
        preferred_element_type=F32,
    )
    own = lax.broadcasted_iota(jnp.int32, (picks, pairs), 1) % picks == lax.broadcasted_iota(
        jnp.int32, (picks, pairs), 0
    )
    wts = jnp.sum(jnp.where(own, tables[:picks], 0.0), axis=0, keepdims=True)
    ids = jnp.sum(jnp.where(own, tables[picks:], 0.0), axis=0, keepdims=True).astype(jnp.int32)
    experts = nodes * locals_
    mine = lax.broadcasted_iota(jnp.int32, (experts, pairs), 0) == ids
    mine_f = jnp.where(mine, 1.0, 0.0)
    before = lax.broadcasted_iota(jnp.int32, (pairs, pairs), 0) < lax.broadcasted_iota(
        jnp.int32, (pairs, pairs), 1
    )
    running = jnp.dot(
        mine_f.astype(BF16), jnp.where(before, 1.0, 0.0).astype(BF16), preferred_element_type=F32
    )
    place = jnp.sum(mine_f * running, axis=0, keepdims=True).astype(jnp.int32)
    slot = ids * cap + place
    hot[...] = jnp.where(
        lax.broadcasted_iota(jnp.int32, (slots, pairs), 0) == slot, 1.0, 0.0
    ).astype(BF16)
    xs[...] = (
        jnp.dot(hot[...], hid_ref[...], preferred_element_type=F32).astype(BF16).reshape(xs.shape)
    )
    spread = jnp.where(lay, wts, 0.0).astype(BF16)
    mix_all = lax.dot_general(
        spread, hot[...], (((1,), (1,)), ((), ())), preferred_element_type=F32
    ).astype(BF16)
    span = nodes * cap
    for l in range(locals_):
        mix[l] = mix_all[:, l * span:(l + 1) * span]

    pl.semaphore_wait(barrier, nodes * locals_ - 1)

    order = list(range(nodes - 1, -1, -1))
    order = [d for d in order if d >= 2] + [d for d in order if d < 2]

    def hidden_copy(d, dl):
        n_t, l_t = node_to(d), local_to(dl)
        return pltpu.make_async_remote_copy(
            src_ref=xs.at[l_t * nodes + n_t], dst_ref=xr.at[d, me_l],
            send_sem=xsend.at[d, dl], recv_sem=xrecv.at[d, dl],
            device_id={"node": n_t, "local": l_t}, device_id_type=MESH,
        )

    def mix_copy(dl):
        l_t = local_to(dl)
        return pltpu.make_async_remote_copy(
            src_ref=mix.at[l_t], dst_ref=mixr.at[me_l],
            send_sem=asend.at[dl], recv_sem=arecv.at[dl],
            device_id={"node": me_n, "local": l_t}, device_id_type=MESH,
        )

    for d in order:
        for dl in range(locals_ - 1, -1, -1):
            if d or dl:
                hidden_copy(d, dl).start()
    for dl in range(1, locals_):
        mix_copy(dl).start()
    xr[0, me_l] = xs[me_l * nodes + me_n]
    mixr[me_l] = mix[me_l]
    weight_copy.wait()

    def return_copy(c, d):
        return pltpu.make_async_remote_copy(
            src_ref=outb.at[c, d],
            dst_ref=zb.at[c, :, pl.ds(pl.multiple_of(me_n * cap, cap), cap), :],
            send_sem=zsend.at[c, d], recv_sem=zrecv.at[c, d],
            device_id={"node": node_from(d), "local": me_l}, device_id_type=MESH,
        )

    side = me_l // 2
    mate = me_l + 1 - 2 * (me_l % 2)
    inner = me_l == 1 + side
    edge = me_l != 1 + side
    away = (1 - side) * 2

    def mate_copy(c):
        return pltpu.make_async_remote_copy(
            src_ref=pb.at[c, mate], dst_ref=rb.at[c, 0],
            send_sem=psend.at[c, 0], recv_sem=precv.at[c, 0],
            device_id={"node": me_n, "local": mate}, device_id_type=MESH,
        )

    def forward_copy(c):
        return pltpu.make_async_remote_copy(
            src_ref=pb.at[c, pl.ds(away, 2)], dst_ref=mb.at[c],
            send_sem=psend.at[c, 1], recv_sem=precv.at[c, 1],
            device_id={"node": me_n, "local": mate}, device_id_type=MESH,
        )

    def cross_copy(c, t):
        return pltpu.make_async_remote_copy(
            src_ref=mb.at[c, t], dst_ref=rb.at[c, 1],
            send_sem=psend.at[c, 2 + t], recv_sem=precv.at[c, 2],
            device_id={"node": me_n, "local": away + t}, device_id_type=MESH,
        )

    lows = list(range(2, nodes, 2)) + [0]

    def hidden_wait(low):
        for d in (low, low + 1):
            for dl in range(locals_):
                if d or dl:
                    hidden_copy(d, dl).wait_recv()

    def apply(c, low):
        cols = pl.ds(pl.multiple_of(c * chunk, chunk), chunk)
        x = xr[low:low + 2].reshape(2 * locals_ * cap, xr.shape[-1])
        o = jnp.dot(x, wv[:, cols], preferred_element_type=F32).astype(BF16)
        o = o.reshape(2, locals_, cap, chunk)
        for k in range(2):
            if low + k:
                outb[c, low + k] = o[k]
                return_copy(c, low + k).start()
            else:
                zb[c, :, pl.ds(pl.multiple_of(me_n * cap, cap), cap), :] = o[k]

    ahead = min(5, chunks)
    for low in lows:
        hidden_wait(low)

        def early_chunk(c, carry, low=low):
            apply(c, low)
            return carry

        lax.fori_loop(0, ahead, early_chunk, 0)

    for dl in range(1, locals_):
        mix_copy(dl).wait_recv()

    def combine(c):
        for d in range(1, nodes):
            return_copy(c, d).wait_recv()
        for l in range(locals_):
            pb[c, l] = jnp.dot(mixr[l], zb[c, l], preferred_element_type=F32).astype(BF16)

        @pl.when(edge)
        def _():
            forward_copy(c).start()

        mate_copy(c).start()

    def merge(c):
        @pl.when(inner)
        def _():
            forward_copy(c).wait_recv()
            for t in range(2):
                mb[c, t] = (mb[c, t].astype(F32) + pb[c, away + t].astype(F32)).astype(BF16)
                cross_copy(c, t).start()

    def combine_chunk(c, carry):
        combine(c)

        @pl.when(c + ahead < chunks)
        def _():
            for low in lows:
                apply(c + ahead, low)

        @pl.when(c > 0)
        def _():
            merge(c - 1)

        return carry

    lax.fori_loop(0, chunks, combine_chunk, 0)
    merge(chunks - 1)

    def final_chunk(c, carry):
        cols = pl.ds(pl.multiple_of(c * chunk, chunk), chunk)
        mate_copy(c).wait_recv()
        cross_copy(c, 0).wait_recv()
        total = pb[c, me_l].astype(F32) + rb[c, 0].astype(F32) + rb[c, 1].astype(F32)
        out_ref[:, cols] = total.astype(BF16)
        return carry

    lax.fori_loop(0, chunks, final_chunk, 0)

    for d in range(nodes):
        for dl in range(locals_):
            if d or dl:
                hidden_copy(d, dl).wait_send()
    for dl in range(1, locals_):
        mix_copy(dl).wait_send()

    def drain(c, carry):
        for d in range(1, nodes):
            return_copy(c, d).wait_send()
        mate_copy(c).wait_send()

        @pl.when(edge)
        def _():
            forward_copy(c).wait_send()

        @pl.when(inner)
        def _():
            for t in range(2):
                cross_copy(c, t).wait_send()

        return carry

    lax.fori_loop(0, chunks, drain, 0)


def dense_plan(hidden, gates, node_groups, group_picks, down_weight, capacity):
    row_count, pick_count, hidden_width = hidden.shape
    nodes = lax.axis_size("node")
    locals_ = lax.axis_size("local")
    width = down_weight.shape[2]
    pairs = row_count * pick_count
    chunk = 256 if width % 256 == 0 else 128
    chunks = width // chunk
    dma = pltpu.SemaphoreType.DMA
    vmem = pl.BlockSpec(memory_space=pltpu.VMEM)
    return pl.pallas_call(
        functools.partial(fused_kernel, nodes, locals_, capacity, chunk),
        out_shape=jax.ShapeDtypeStruct((row_count, width), BF16),
        in_specs=[vmem, vmem, vmem, vmem, pl.BlockSpec(memory_space=pl.ANY)],
        out_specs=vmem,
        scratch_shapes=[
            pltpu.VMEM((nodes * locals_ * capacity, pairs), BF16),
            pltpu.VMEM((nodes * locals_, capacity, hidden_width), BF16),
            pltpu.VMEM((nodes, locals_, capacity, hidden_width), BF16),
            pltpu.VMEM((locals_, row_count, nodes * capacity), BF16),
            pltpu.VMEM((locals_, row_count, nodes * capacity), BF16),
            pltpu.VMEM((hidden_width, width), BF16),
            pltpu.VMEM((chunks, nodes, locals_, capacity, chunk), BF16),
            pltpu.VMEM((chunks, locals_, nodes * capacity, chunk), BF16),
            pltpu.VMEM((chunks, locals_, row_count, chunk), BF16),
            pltpu.VMEM((chunks, 2, row_count, chunk), BF16),
            pltpu.VMEM((chunks, 2, row_count, chunk), BF16),
            dma,
            dma((nodes, locals_)),
            dma((nodes, locals_)),
            dma((locals_,)),
            dma((locals_,)),
            dma((chunks, nodes)),
            dma((chunks, nodes)),
            dma((chunks, 4)),
            dma((chunks, 3)),
        ],
        compiler_params=pltpu.CompilerParams(
            collective_id=0, has_side_effects=True, vmem_limit_bytes=56 * 1024 * 1024
        ),
    )(
        gates.T,
        node_groups.T,
        group_picks.T,
        hidden.reshape(pairs, hidden_width),
        down_weight,
    )


def shards(hidden, gates, node_groups, group_picks, down_weight):
    row_count = hidden.shape[0]
    nodes = lax.axis_size("node")
    capacity = 2 * row_count // lax.axis_size("local")
    if nodes == node_groups.shape[1] and nodes % 2 == 0 and lax.axis_size("local") == 4:
        return dense_plan(hidden, gates, node_groups, group_picks, down_weight, capacity)
    route_weights = (route_scale * gates / jnp.sum(gates, axis=1, keepdims=True)).astype(BF16)
    return sparse_plan(
        hidden, route_weights, node_groups, group_picks, down_weight[0], capacity
    )


def solution(mesh):
    return jax.shard_map(
        shards,
        mesh=mesh,
        in_specs=(
            P(("groups", "node", "local"), None, None),
            P(("groups", "node", "local"), None),
            P(("groups", "node", "local"), None),
            P(("groups", "node", "local"), None),
            P(("node", "local"), None, None),
        ),
        out_specs=P(("groups", "node", "local"), None),
        check_vma=False,
    )
```

```python
import functools

import jax
import jax.numpy as jnp
from jax import lax
from jax.experimental import pallas as pl
from jax.experimental.pallas import tpu as pltpu
from jax.sharding import PartitionSpec as P

route_scale = 2.5
MESH = pl.DeviceIdType.MESH
BF16 = jnp.bfloat16
F32 = jnp.float32


def expert_apply(inputs, weight_block):
    flat_rows = inputs.reshape(-1, inputs.shape[-1])
    product = jnp.dot(flat_rows, weight_block, preferred_element_type=jnp.float32)
    return product.astype(jnp.bfloat16).reshape(inputs.shape[:-1] + (weight_block.shape[1],))


def slot_positions(targets, count):
    one_hot = (targets[:, None] == jnp.arange(count, dtype=jnp.int32)[None, :]).astype(jnp.int32)
    running = jnp.cumsum(one_hot, axis=0) - 1
    return jnp.sum(running * one_hot, axis=1)


def pack_rows(hidden, node_groups, pair_picks, local_count, device_count, capacity):
    hidden_width = hidden.shape[2]
    expert_ids = (node_groups[:, :, None] * local_count + pair_picks).reshape(-1)
    slot_index = expert_ids * capacity + slot_positions(expert_ids, device_count)
    outgoing = (
        jnp.zeros((device_count * capacity, hidden_width), jnp.bfloat16)
        .at[slot_index]
        .set(hidden.reshape(-1, hidden_width))
    )
    return (slot_index, outgoing)


def combine_rows(returned, slot_index, pair_weights):
    row_count, group_count, pair_count = pair_weights.shape
    model_width = returned.shape[-1]
    picked = returned.reshape(-1, model_width)[slot_index].astype(jnp.float32)
    picked = picked.reshape(row_count, group_count, pair_count, model_width)
    group_sums = jnp.sum(pair_weights.astype(jnp.float32)[..., None] * picked, axis=2).astype(
        jnp.bfloat16
    )
    return jnp.sum(group_sums.astype(jnp.float32), axis=1).astype(jnp.bfloat16)


def sparse_plan(hidden, route_weights, node_groups, group_picks, weight_block, capacity):
    row_count, pick_count, hidden_width = hidden.shape
    group_count = node_groups.shape[1]
    pair_count = pick_count // group_count
    local_count = lax.axis_size("local")
    device_count = lax.axis_size("node") * local_count
    pair_weights = route_weights.reshape(row_count, group_count, pair_count)
    pair_picks = group_picks.reshape(row_count, group_count, pair_count)
    slot_index, outgoing = pack_rows(
        hidden, node_groups, pair_picks, local_count, device_count, capacity
    )
    arrived = lax.all_to_all(
        outgoing.reshape(device_count, capacity, hidden_width),
        ("node", "local"),
        split_axis=0,
        concat_axis=0,
        tiled=True,
    )
    returned = lax.all_to_all(
        expert_apply(arrived, weight_block),
        ("node", "local"),
        split_axis=0,
        concat_axis=0,
        tiled=True,
    )
    return combine_rows(returned, slot_index, pair_weights)


def fused_kernel(
    nodes, locals_, cap, chunk,
    gates_ref, groups_ref, picks_ref, hid_ref, w_hbm, out_ref,
    hot, xs, xr, mix, mixr, wv, outb, zb, pb, mb, rb,
    w_sem, xsend, xrecv, asend, arecv, zsend, zrecv, psend, precv,
):
    half = nodes // 2
    me_n = lax.axis_index("node")
    me_l = lax.axis_index("local")
    me_y, me_c = me_n // 2, me_n % 2
    rows, width = out_ref.shape
    picks, pairs = gates_ref.shape[0], hid_ref.shape[0]
    share = picks // groups_ref.shape[0]
    slots = nodes * locals_ * cap
    chunks = width // chunk

    def node_to(d):
        return ((me_y + d // 2) % half) * 2 + (me_c + d % 2) % 2

    def node_from(d):
        return ((me_y - d // 2 + half) % half) * 2 + (me_c - d % 2 + 2) % 2

    def local_to(d):
        return (me_l + d) % locals_

    barrier = pltpu.get_barrier_semaphore()
    for d in range(nodes):
        for dl in range(locals_):
            if d or dl:
                pl.semaphore_signal(
                    barrier, inc=1, device_id={"node": node_to(d), "local": local_to(dl)},
                    device_id_type=MESH,
                )

    weight_copy = pltpu.make_async_copy(w_hbm.at[0], wv, w_sem)
    weight_copy.start()

    gates = gates_ref[...]
    weights = route_scale * gates / jnp.sum(gates, axis=0, keepdims=True)
    groups = jnp.concatenate(
        [groups_ref[j // share:j // share + 1, :] for j in range(picks)], axis=0
    )
    numbers = (picks_ref[...] * nodes + groups).astype(F32)
    lay = lax.broadcasted_iota(jnp.int32, (rows, pairs), 1) // picks == lax.broadcasted_iota(
        jnp.int32, (rows, pairs), 0
    )
    tables = jnp.dot(
        jnp.concatenate([weights, numbers], axis=0).astype(BF16),
        jnp.where(lay, 1.0, 0.0).astype(BF16),
        preferred_element_type=F32,
    )
    own = lax.broadcasted_iota(jnp.int32, (picks, pairs), 1) % picks == lax.broadcasted_iota(
        jnp.int32, (picks, pairs), 0
    )
    wts = jnp.sum(jnp.where(own, tables[:picks], 0.0), axis=0, keepdims=True)
    ids = jnp.sum(jnp.where(own, tables[picks:], 0.0), axis=0, keepdims=True).astype(jnp.int32)
    experts = nodes * locals_
    mine = lax.broadcasted_iota(jnp.int32, (experts, pairs), 0) == ids
    mine_f = jnp.where(mine, 1.0, 0.0)
    before = lax.broadcasted_iota(jnp.int32, (pairs, pairs), 0) < lax.broadcasted_iota(
        jnp.int32, (pairs, pairs), 1
    )
    running = jnp.dot(
        mine_f.astype(BF16), jnp.where(before, 1.0, 0.0).astype(BF16), preferred_element_type=F32
    )
    place = jnp.sum(mine_f * running, axis=0, keepdims=True).astype(jnp.int32)
    slot = ids * cap + place
    hot[...] = jnp.where(
        lax.broadcasted_iota(jnp.int32, (slots, pairs), 0) == slot, 1.0, 0.0
    ).astype(BF16)
    xs[...] = (
        jnp.dot(hot[...], hid_ref[...], preferred_element_type=F32).astype(BF16).reshape(xs.shape)
    )

    pl.semaphore_wait(barrier, nodes * locals_ - 1)

    order = list(range(nodes - 1, -1, -1))
    order = [d for d in order if d >= 2] + [d for d in order if d < 2]

    def hidden_copy(d, dl):
        n_t, l_t = node_to(d), local_to(dl)
        return pltpu.make_async_remote_copy(
            src_ref=xs.at[l_t * nodes + n_t], dst_ref=xr.at[d, me_l],
            send_sem=xsend.at[d, dl], recv_sem=xrecv.at[d, dl],
            device_id={"node": n_t, "local": l_t}, device_id_type=MESH,
        )

    def mix_copy(dl):
        l_t = local_to(dl)
        return pltpu.make_async_remote_copy(
            src_ref=mix.at[l_t], dst_ref=mixr.at[me_l],
            send_sem=asend.at[dl], recv_sem=arecv.at[dl],
            device_id={"node": me_n, "local": l_t}, device_id_type=MESH,
        )

    for d in order:
        for dl in range(locals_ - 1, -1, -1):
            if d or dl:
                hidden_copy(d, dl).start()

    spread = jnp.where(lay, wts, 0.0).astype(BF16)
    mix_all = lax.dot_general(
        spread, hot[...], (((1,), (1,)), ((), ())), preferred_element_type=F32
    ).astype(BF16)
    span = nodes * cap
    for l in range(locals_):
        mix[l] = mix_all[:, l * span:(l + 1) * span]
    for dl in range(1, locals_):
        mix_copy(dl).start()
    xr[0, me_l] = xs[me_l * nodes + me_n]
    mixr[me_l] = mix[me_l]
    weight_copy.wait()

    def return_copy(c, d):
        return pltpu.make_async_remote_copy(
            src_ref=outb.at[c, d],
            dst_ref=zb.at[c, :, pl.ds(pl.multiple_of(me_n * cap, cap), cap), :],
            send_sem=zsend.at[c, d], recv_sem=zrecv.at[c, d],
            device_id={"node": node_from(d), "local": me_l}, device_id_type=MESH,
        )

    side = me_l // 2
    mate = me_l + 1 - 2 * (me_l % 2)
    inner = me_l == 1 + side
    edge = me_l != 1 + side
    away = (1 - side) * 2

    def mate_copy(c):
        return pltpu.make_async_remote_copy(
            src_ref=pb.at[c, mate], dst_ref=rb.at[c, 0],
            send_sem=psend.at[c, 0], recv_sem=precv.at[c, 0],
            device_id={"node": me_n, "local": mate}, device_id_type=MESH,
        )

    def forward_copy(c):
        return pltpu.make_async_remote_copy(
            src_ref=pb.at[c, pl.ds(away, 2)], dst_ref=mb.at[c],
            send_sem=psend.at[c, 1], recv_sem=precv.at[c, 1],
            device_id={"node": me_n, "local": mate}, device_id_type=MESH,
        )

    def cross_copy(c, t):
        return pltpu.make_async_remote_copy(
            src_ref=mb.at[c, t], dst_ref=rb.at[c, 1],
            send_sem=psend.at[c, 2 + t], recv_sem=precv.at[c, 2],
            device_id={"node": me_n, "local": away + t}, device_id_type=MESH,
        )

    lows = list(range(2, nodes, 2)) + [0]

    def hidden_wait(low):
        for d in (low, low + 1):
            for dl in range(locals_):
                if d or dl:
                    hidden_copy(d, dl).wait_recv()

    def apply(c, low):
        cols = pl.ds(pl.multiple_of(c * chunk, chunk), chunk)
        x = xr[low:low + 2].reshape(2 * locals_ * cap, xr.shape[-1])
        o = jnp.dot(x, wv[:, cols], preferred_element_type=F32).astype(BF16)
        o = o.reshape(2, locals_, cap, chunk)
        for k in range(2):
            if low + k:
                outb[c, low + k] = o[k]
                return_copy(c, low + k).start()
            else:
                zb[c, :, pl.ds(pl.multiple_of(me_n * cap, cap), cap), :] = o[k]

    ahead = min(5, chunks)
    for low in lows:
        hidden_wait(low)

        def early_chunk(c, carry, low=low):
            apply(c, low)
            return carry

        lax.fori_loop(0, ahead, early_chunk, 0)

    for dl in range(1, locals_):
        mix_copy(dl).wait_recv()

    def combine(c):
        for d in range(1, nodes):
            return_copy(c, d).wait_recv()
        for l in range(locals_):
            pb[c, l] = jnp.dot(mixr[l], zb[c, l], preferred_element_type=F32).astype(BF16)

        @pl.when(edge)
        def _():
            forward_copy(c).start()

        mate_copy(c).start()

    def merge(c):
        @pl.when(inner)
        def _():
            forward_copy(c).wait_recv()
            for t in range(2):
                mb[c, t] = (mb[c, t].astype(F32) + pb[c, away + t].astype(F32)).astype(BF16)
                cross_copy(c, t).start()

    def combine_chunk(c, carry):
        combine(c)

        @pl.when(c + ahead < chunks)
        def _():
            for low in lows:
                apply(c + ahead, low)

        @pl.when(c > 0)
        def _():
            merge(c - 1)

        return carry

    lax.fori_loop(0, chunks, combine_chunk, 0)
    merge(chunks - 1)

    def final_chunk(c, carry):
        cols = pl.ds(pl.multiple_of(c * chunk, chunk), chunk)
        mate_copy(c).wait_recv()
        cross_copy(c, 0).wait_recv()
        total = pb[c, me_l].astype(F32) + rb[c, 0].astype(F32) + rb[c, 1].astype(F32)
        out_ref[:, cols] = total.astype(BF16)
        return carry

    lax.fori_loop(0, chunks, final_chunk, 0)

    for d in range(nodes):
        for dl in range(locals_):
            if d or dl:
                hidden_copy(d, dl).wait_send()
    for dl in range(1, locals_):
        mix_copy(dl).wait_send()

    def drain(c, carry):
        for d in range(1, nodes):
            return_copy(c, d).wait_send()
        mate_copy(c).wait_send()

        @pl.when(edge)
        def _():
            forward_copy(c).wait_send()

        @pl.when(inner)
        def _():
            for t in range(2):
                cross_copy(c, t).wait_send()

        return carry

    lax.fori_loop(0, chunks, drain, 0)


def dense_plan(hidden, gates, node_groups, group_picks, down_weight, capacity):
    row_count, pick_count, hidden_width = hidden.shape
    nodes = lax.axis_size("node")
    locals_ = lax.axis_size("local")
    width = down_weight.shape[2]
    pairs = row_count * pick_count
    chunk = 256 if width % 256 == 0 else 128
    chunks = width // chunk
    dma = pltpu.SemaphoreType.DMA
    vmem = pl.BlockSpec(memory_space=pltpu.VMEM)
    return pl.pallas_call(
        functools.partial(fused_kernel, nodes, locals_, capacity, chunk),
        out_shape=jax.ShapeDtypeStruct((row_count, width), BF16),
        in_specs=[vmem, vmem, vmem, vmem, pl.BlockSpec(memory_space=pl.ANY)],
        out_specs=vmem,
        scratch_shapes=[
            pltpu.VMEM((nodes * locals_ * capacity, pairs), BF16),
            pltpu.VMEM((nodes * locals_, capacity, hidden_width), BF16),
            pltpu.VMEM((nodes, locals_, capacity, hidden_width), BF16),
            pltpu.VMEM((locals_, row_count, nodes * capacity), BF16),
            pltpu.VMEM((locals_, row_count, nodes * capacity), BF16),
            pltpu.VMEM((hidden_width, width), BF16),
            pltpu.VMEM((chunks, nodes, locals_, capacity, chunk), BF16),
            pltpu.VMEM((chunks, locals_, nodes * capacity, chunk), BF16),
            pltpu.VMEM((chunks, locals_, row_count, chunk), BF16),
            pltpu.VMEM((chunks, 2, row_count, chunk), BF16),
            pltpu.VMEM((chunks, 2, row_count, chunk), BF16),
            dma,
            dma((nodes, locals_)),
            dma((nodes, locals_)),
            dma((locals_,)),
            dma((locals_,)),
            dma((chunks, nodes)),
            dma((chunks, nodes)),
            dma((chunks, 4)),
            dma((chunks, 3)),
        ],
        compiler_params=pltpu.CompilerParams(
            collective_id=0, has_side_effects=True, vmem_limit_bytes=56 * 1024 * 1024
        ),
    )(
        gates.T,
        node_groups.T,
        group_picks.T,
        hidden.reshape(pairs, hidden_width),
        down_weight,
    )


def shards(hidden, gates, node_groups, group_picks, down_weight):
    row_count = hidden.shape[0]
    nodes = lax.axis_size("node")
    capacity = 2 * row_count // lax.axis_size("local")
    if nodes == node_groups.shape[1] and nodes % 2 == 0 and lax.axis_size("local") == 4:
        return dense_plan(hidden, gates, node_groups, group_picks, down_weight, capacity)
    route_weights = (route_scale * gates / jnp.sum(gates, axis=1, keepdims=True)).astype(BF16)
    return sparse_plan(
        hidden, route_weights, node_groups, group_picks, down_weight[0], capacity
    )


def solution(mesh):
    return jax.shard_map(
        shards,
        mesh=mesh,
        in_specs=(
            P(("groups", "node", "local"), None, None),
            P(("groups", "node", "local"), None),
            P(("groups", "node", "local"), None),
            P(("groups", "node", "local"), None),
            P(("node", "local"), None, None),
        ),
        out_specs=P(("groups", "node", "local"), None),
        check_vma=False,
    )
```

```python
import functools

import jax
import jax.numpy as jnp
from jax import lax
from jax.experimental import pallas as pl
from jax.experimental.pallas import tpu as pltpu
from jax.sharding import PartitionSpec as P

route_scale = 2.5
MESH = pl.DeviceIdType.MESH
BF16 = jnp.bfloat16
F32 = jnp.float32


def expert_apply(inputs, weight_block):
    flat_rows = inputs.reshape(-1, inputs.shape[-1])
    product = jnp.dot(flat_rows, weight_block, preferred_element_type=jnp.float32)
    return product.astype(jnp.bfloat16).reshape(inputs.shape[:-1] + (weight_block.shape[1],))


def slot_positions(targets, count):
    one_hot = (targets[:, None] == jnp.arange(count, dtype=jnp.int32)[None, :]).astype(jnp.int32)
    running = jnp.cumsum(one_hot, axis=0) - 1
    return jnp.sum(running * one_hot, axis=1)


def pack_rows(hidden, node_groups, pair_picks, local_count, device_count, capacity):
    hidden_width = hidden.shape[2]
    expert_ids = (node_groups[:, :, None] * local_count + pair_picks).reshape(-1)
    slot_index = expert_ids * capacity + slot_positions(expert_ids, device_count)
    outgoing = (
        jnp.zeros((device_count * capacity, hidden_width), jnp.bfloat16)
        .at[slot_index]
        .set(hidden.reshape(-1, hidden_width))
    )
    return (slot_index, outgoing)


def combine_rows(returned, slot_index, pair_weights):
    row_count, group_count, pair_count = pair_weights.shape
    model_width = returned.shape[-1]
    picked = returned.reshape(-1, model_width)[slot_index].astype(jnp.float32)
    picked = picked.reshape(row_count, group_count, pair_count, model_width)
    group_sums = jnp.sum(pair_weights.astype(jnp.float32)[..., None] * picked, axis=2).astype(
        jnp.bfloat16
    )
    return jnp.sum(group_sums.astype(jnp.float32), axis=1).astype(jnp.bfloat16)


def sparse_plan(hidden, route_weights, node_groups, group_picks, weight_block, capacity):
    row_count, pick_count, hidden_width = hidden.shape
    group_count = node_groups.shape[1]
    pair_count = pick_count // group_count
    local_count = lax.axis_size("local")
    device_count = lax.axis_size("node") * local_count
    pair_weights = route_weights.reshape(row_count, group_count, pair_count)
    pair_picks = group_picks.reshape(row_count, group_count, pair_count)
    slot_index, outgoing = pack_rows(
        hidden, node_groups, pair_picks, local_count, device_count, capacity
    )
    arrived = lax.all_to_all(
        outgoing.reshape(device_count, capacity, hidden_width),
        ("node", "local"),
        split_axis=0,
        concat_axis=0,
        tiled=True,
    )
    returned = lax.all_to_all(
        expert_apply(arrived, weight_block),
        ("node", "local"),
        split_axis=0,
        concat_axis=0,
        tiled=True,
    )
    return combine_rows(returned, slot_index, pair_weights)


def fused_kernel(
    nodes, locals_, cap, chunk,
    gates_ref, groups_ref, picks_ref, hid_ref, w_hbm, out_ref,
    hot, xs, xr, mix, mixr, wv, outb, zb, pb, mb, rb,
    w_sem, xsend, xrecv, asend, arecv, zsend, zrecv, psend, precv,
):
    half = nodes // 2
    me_n = lax.axis_index("node")
    me_l = lax.axis_index("local")
    me_y, me_c = me_n // 2, me_n % 2
    rows, width = out_ref.shape
    picks, pairs = gates_ref.shape[0], hid_ref.shape[0]
    share = picks // groups_ref.shape[0]
    slots = nodes * locals_ * cap
    chunks = width // chunk

    def node_to(d):
        return ((me_y + d // 2) % half) * 2 + (me_c + d % 2) % 2

    def node_from(d):
        return ((me_y - d // 2 + half) % half) * 2 + (me_c - d % 2 + 2) % 2

    def local_to(d):
        return (me_l + d) % locals_

    barrier = pltpu.get_barrier_semaphore()
    for d in range(nodes):
        for dl in range(locals_):
            if d or dl:
                pl.semaphore_signal(
                    barrier, inc=1, device_id={"node": node_to(d), "local": local_to(dl)},
                    device_id_type=MESH,
                )

    weight_copy = pltpu.make_async_copy(w_hbm.at[0], wv, w_sem)
    weight_copy.start()

    gates = gates_ref[...]
    weights = route_scale * gates / jnp.sum(gates, axis=0, keepdims=True)
    groups = jnp.concatenate(
        [groups_ref[j // share:j // share + 1, :] for j in range(picks)], axis=0
    )
    numbers = (picks_ref[...] * nodes + groups).astype(F32)
    lay = lax.broadcasted_iota(jnp.int32, (rows, pairs), 1) // picks == lax.broadcasted_iota(
        jnp.int32, (rows, pairs), 0
    )
    tables = jnp.dot(
        jnp.concatenate([weights, numbers], axis=0).astype(BF16),
        jnp.where(lay, 1.0, 0.0).astype(BF16),
        preferred_element_type=F32,
    )
    own = lax.broadcasted_iota(jnp.int32, (picks, pairs), 1) % picks == lax.broadcasted_iota(
        jnp.int32, (picks, pairs), 0
    )
    wts = jnp.sum(jnp.where(own, tables[:picks], 0.0), axis=0, keepdims=True)
    ids = jnp.sum(jnp.where(own, tables[picks:], 0.0), axis=0, keepdims=True).astype(jnp.int32)
    experts = nodes * locals_
    mine = lax.broadcasted_iota(jnp.int32, (experts, pairs), 0) == ids
    mine_f = jnp.where(mine, 1.0, 0.0)
    before = lax.broadcasted_iota(jnp.int32, (pairs, pairs), 0) < lax.broadcasted_iota(
        jnp.int32, (pairs, pairs), 1
    )
    running = jnp.dot(
        mine_f.astype(BF16), jnp.where(before, 1.0, 0.0).astype(BF16), preferred_element_type=F32
    )
    place = jnp.sum(mine_f * running, axis=0, keepdims=True).astype(jnp.int32)
    slot = ids * cap + place
    hot[...] = jnp.where(
        lax.broadcasted_iota(jnp.int32, (slots, pairs), 0) == slot, 1.0, 0.0
    ).astype(BF16)
    xs[...] = (
        jnp.dot(hot[...], hid_ref[...], preferred_element_type=F32).astype(BF16).reshape(xs.shape)
    )
    spread = jnp.where(lay, wts, 0.0).astype(BF16)
    mix_all = lax.dot_general(
        spread, hot[...], (((1,), (1,)), ((), ())), preferred_element_type=F32
    ).astype(BF16)
    span = nodes * cap
    for l in range(locals_):
        mix[l] = mix_all[:, l * span:(l + 1) * span]

    pl.semaphore_wait(barrier, nodes * locals_ - 1)

    order = list(range(nodes - 1, -1, -1))
    order = [d for d in order if d >= 2] + [d for d in order if d < 2]

    def hidden_copy(d, dl):
        n_t, l_t = node_to(d), local_to(dl)
        return pltpu.make_async_remote_copy(
            src_ref=xs.at[l_t * nodes + n_t], dst_ref=xr.at[d, me_l],
            send_sem=xsend.at[d, dl], recv_sem=xrecv.at[d, dl],
            device_id={"node": n_t, "local": l_t}, device_id_type=MESH,
        )

    def mix_copy(dl):
        l_t = local_to(dl)
        return pltpu.make_async_remote_copy(
            src_ref=mix.at[l_t], dst_ref=mixr.at[me_l],
            send_sem=asend.at[dl], recv_sem=arecv.at[dl],
            device_id={"node": me_n, "local": l_t}, device_id_type=MESH,
        )

    for k in range(0, nodes, 2):
        for dl in (2, 1, 3, 0):
            for d in order[k:k + 2]:
                if d or dl:
                    hidden_copy(d, dl).start()
    for dl in range(1, locals_):
        mix_copy(dl).start()
    xr[0, me_l] = xs[me_l * nodes + me_n]
    mixr[me_l] = mix[me_l]
    weight_copy.wait()

    def return_copy(c, d):
        return pltpu.make_async_remote_copy(
            src_ref=outb.at[c, d],
            dst_ref=zb.at[c, :, pl.ds(pl.multiple_of(me_n * cap, cap), cap), :],
            send_sem=zsend.at[c, d], recv_sem=zrecv.at[c, d],
            device_id={"node": node_from(d), "local": me_l}, device_id_type=MESH,
        )

    side = me_l // 2
    mate = me_l + 1 - 2 * (me_l % 2)
    inner = me_l == 1 + side
    edge = me_l != 1 + side
    away = (1 - side) * 2

    def mate_copy(c):
        return pltpu.make_async_remote_copy(
            src_ref=pb.at[c, mate], dst_ref=rb.at[c, 0],
            send_sem=psend.at[c, 0], recv_sem=precv.at[c, 0],
            device_id={"node": me_n, "local": mate}, device_id_type=MESH,
        )

    def forward_copy(c):
        return pltpu.make_async_remote_copy(
            src_ref=pb.at[c, pl.ds(away, 2)], dst_ref=mb.at[c],
            send_sem=psend.at[c, 1], recv_sem=precv.at[c, 1],
            device_id={"node": me_n, "local": mate}, device_id_type=MESH,
        )

    def cross_copy(c, t):
        return pltpu.make_async_remote_copy(
            src_ref=mb.at[c, t], dst_ref=rb.at[c, 1],
            send_sem=psend.at[c, 2 + t], recv_sem=precv.at[c, 2],
            device_id={"node": me_n, "local": away + t}, device_id_type=MESH,
        )

    lows = list(range(2, nodes, 2)) + [0]

    def hidden_wait(low):
        for d in (low, low + 1):
            for dl in range(locals_):
                if d or dl:
                    hidden_copy(d, dl).wait_recv()

    def apply(c, low):
        cols = pl.ds(pl.multiple_of(c * chunk, chunk), chunk)
        x = xr[low:low + 2].reshape(2 * locals_ * cap, xr.shape[-1])
        o = jnp.dot(x, wv[:, cols], preferred_element_type=F32).astype(BF16)
        o = o.reshape(2, locals_, cap, chunk)
        for k in range(2):
            if low + k:
                outb[c, low + k] = o[k]
                return_copy(c, low + k).start()
            else:
                zb[c, :, pl.ds(pl.multiple_of(me_n * cap, cap), cap), :] = o[k]

    ahead = min(5, chunks)
    for low in lows:
        hidden_wait(low)

        def early_chunk(c, carry, low=low):
            apply(c, low)
            return carry

        lax.fori_loop(0, ahead, early_chunk, 0)

    for dl in range(1, locals_):
        mix_copy(dl).wait_recv()

    def combine(c):
        for d in range(1, nodes):
            return_copy(c, d).wait_recv()
        for l in range(locals_):
            pb[c, l] = jnp.dot(mixr[l], zb[c, l], preferred_element_type=F32).astype(BF16)

        @pl.when(edge)
        def _():
            forward_copy(c).start()

        mate_copy(c).start()

    def merge(c):
        @pl.when(inner)
        def _():
            forward_copy(c).wait_recv()
            for t in range(2):
                mb[c, t] = (mb[c, t].astype(F32) + pb[c, away + t].astype(F32)).astype(BF16)
                cross_copy(c, t).start()

    def combine_chunk(c, carry):
        combine(c)

        @pl.when(c + ahead < chunks)
        def _():
            for low in lows:
                apply(c + ahead, low)

        @pl.when(c > 0)
        def _():
            merge(c - 1)

        return carry

    lax.fori_loop(0, chunks, combine_chunk, 0)
    merge(chunks - 1)

    def final_chunk(c, carry):
        cols = pl.ds(pl.multiple_of(c * chunk, chunk), chunk)
        mate_copy(c).wait_recv()
        cross_copy(c, 0).wait_recv()
        total = pb[c, me_l].astype(F32) + rb[c, 0].astype(F32) + rb[c, 1].astype(F32)
        out_ref[:, cols] = total.astype(BF16)
        return carry

    lax.fori_loop(0, chunks, final_chunk, 0)

    for d in range(nodes):
        for dl in range(locals_):
            if d or dl:
                hidden_copy(d, dl).wait_send()
    for dl in range(1, locals_):
        mix_copy(dl).wait_send()

    def drain(c, carry):
        for d in range(1, nodes):
            return_copy(c, d).wait_send()
        mate_copy(c).wait_send()

        @pl.when(edge)
        def _():
            forward_copy(c).wait_send()

        @pl.when(inner)
        def _():
            for t in range(2):
                cross_copy(c, t).wait_send()

        return carry

    lax.fori_loop(0, chunks, drain, 0)


def dense_plan(hidden, gates, node_groups, group_picks, down_weight, capacity):
    row_count, pick_count, hidden_width = hidden.shape
    nodes = lax.axis_size("node")
    locals_ = lax.axis_size("local")
    width = down_weight.shape[2]
    pairs = row_count * pick_count
    chunk = 256 if width % 256 == 0 else 128
    chunks = width // chunk
    dma = pltpu.SemaphoreType.DMA
    vmem = pl.BlockSpec(memory_space=pltpu.VMEM)
    return pl.pallas_call(
        functools.partial(fused_kernel, nodes, locals_, capacity, chunk),
        out_shape=jax.ShapeDtypeStruct((row_count, width), BF16),
        in_specs=[vmem, vmem, vmem, vmem, pl.BlockSpec(memory_space=pl.ANY)],
        out_specs=vmem,
        scratch_shapes=[
            pltpu.VMEM((nodes * locals_ * capacity, pairs), BF16),
            pltpu.VMEM((nodes * locals_, capacity, hidden_width), BF16),
            pltpu.VMEM((nodes, locals_, capacity, hidden_width), BF16),
            pltpu.VMEM((locals_, row_count, nodes * capacity), BF16),
            pltpu.VMEM((locals_, row_count, nodes * capacity), BF16),
            pltpu.VMEM((hidden_width, width), BF16),
            pltpu.VMEM((chunks, nodes, locals_, capacity, chunk), BF16),
            pltpu.VMEM((chunks, locals_, nodes * capacity, chunk), BF16),
            pltpu.VMEM((chunks, locals_, row_count, chunk), BF16),
            pltpu.VMEM((chunks, 2, row_count, chunk), BF16),
            pltpu.VMEM((chunks, 2, row_count, chunk), BF16),
            dma,
            dma((nodes, locals_)),
            dma((nodes, locals_)),
            dma((locals_,)),
            dma((locals_,)),
            dma((chunks, nodes)),
            dma((chunks, nodes)),
            dma((chunks, 4)),
            dma((chunks, 3)),
        ],
        compiler_params=pltpu.CompilerParams(
            collective_id=0, has_side_effects=True, vmem_limit_bytes=56 * 1024 * 1024
        ),
    )(
        gates.T,
        node_groups.T,
        group_picks.T,
        hidden.reshape(pairs, hidden_width),
        down_weight,
    )


def shards(hidden, gates, node_groups, group_picks, down_weight):
    row_count = hidden.shape[0]
    nodes = lax.axis_size("node")
    capacity = 2 * row_count // lax.axis_size("local")
    if nodes == node_groups.shape[1] and nodes % 2 == 0 and lax.axis_size("local") == 4:
        return dense_plan(hidden, gates, node_groups, group_picks, down_weight, capacity)
    route_weights = (route_scale * gates / jnp.sum(gates, axis=1, keepdims=True)).astype(BF16)
    return sparse_plan(
        hidden, route_weights, node_groups, group_picks, down_weight[0], capacity
    )


def solution(mesh):
    return jax.shard_map(
        shards,
        mesh=mesh,
        in_specs=(
            P(("groups", "node", "local"), None, None),
            P(("groups", "node", "local"), None),
            P(("groups", "node", "local"), None),
            P(("groups", "node", "local"), None),
            P(("node", "local"), None, None),
        ),
        out_specs=P(("groups", "node", "local"), None),
        check_vma=False,
    )
```

```python
import functools

import jax
import jax.numpy as jnp
from jax import lax
from jax.experimental import pallas as pl
from jax.experimental.pallas import tpu as pltpu
from jax.sharding import PartitionSpec as P

route_scale = 2.5
MESH = pl.DeviceIdType.MESH
BF16 = jnp.bfloat16
F32 = jnp.float32


def expert_apply(inputs, weight_block):
    flat_rows = inputs.reshape(-1, inputs.shape[-1])
    product = jnp.dot(flat_rows, weight_block, preferred_element_type=jnp.float32)
    return product.astype(jnp.bfloat16).reshape(inputs.shape[:-1] + (weight_block.shape[1],))


def slot_positions(targets, count):
    one_hot = (targets[:, None] == jnp.arange(count, dtype=jnp.int32)[None, :]).astype(jnp.int32)
    running = jnp.cumsum(one_hot, axis=0) - 1
    return jnp.sum(running * one_hot, axis=1)


def pack_rows(hidden, node_groups, pair_picks, local_count, device_count, capacity):
    hidden_width = hidden.shape[2]
    expert_ids = (node_groups[:, :, None] * local_count + pair_picks).reshape(-1)
    slot_index = expert_ids * capacity + slot_positions(expert_ids, device_count)
    outgoing = (
        jnp.zeros((device_count * capacity, hidden_width), jnp.bfloat16)
        .at[slot_index]
        .set(hidden.reshape(-1, hidden_width))
    )
    return (slot_index, outgoing)


def combine_rows(returned, slot_index, pair_weights):
    row_count, group_count, pair_count = pair_weights.shape
    model_width = returned.shape[-1]
    picked = returned.reshape(-1, model_width)[slot_index].astype(jnp.float32)
    picked = picked.reshape(row_count, group_count, pair_count, model_width)
    group_sums = jnp.sum(pair_weights.astype(jnp.float32)[..., None] * picked, axis=2).astype(
        jnp.bfloat16
    )
    return jnp.sum(group_sums.astype(jnp.float32), axis=1).astype(jnp.bfloat16)


def sparse_plan(hidden, route_weights, node_groups, group_picks, weight_block, capacity):
    row_count, pick_count, hidden_width = hidden.shape
    group_count = node_groups.shape[1]
    pair_count = pick_count // group_count
    local_count = lax.axis_size("local")
    device_count = lax.axis_size("node") * local_count
    pair_weights = route_weights.reshape(row_count, group_count, pair_count)
    pair_picks = group_picks.reshape(row_count, group_count, pair_count)
    slot_index, outgoing = pack_rows(
        hidden, node_groups, pair_picks, local_count, device_count, capacity
    )
    arrived = lax.all_to_all(
        outgoing.reshape(device_count, capacity, hidden_width),
        ("node", "local"),
        split_axis=0,
        concat_axis=0,
        tiled=True,
    )
    returned = lax.all_to_all(
        expert_apply(arrived, weight_block),
        ("node", "local"),
        split_axis=0,
        concat_axis=0,
        tiled=True,
    )
    return combine_rows(returned, slot_index, pair_weights)


def fused_kernel(
    nodes, locals_, cap, chunk,
    gates_ref, groups_ref, picks_ref, hid_ref, w_hbm, out_ref,
    hot, xs, xr, mix, mixr, wv, outb, zb, pb, mb, rb,
    w_sem, xsend, xrecv, asend, arecv, zsend, zrecv, psend, precv,
):
    half = nodes // 2
    me_n = lax.axis_index("node")
    me_l = lax.axis_index("local")
    me_y, me_c = me_n // 2, me_n % 2
    rows, width = out_ref.shape
    picks, pairs = gates_ref.shape[0], hid_ref.shape[0]
    share = picks // groups_ref.shape[0]
    slots = nodes * locals_ * cap
    chunks = width // chunk

    def node_to(d):
        return ((me_y + d // 2) % half) * 2 + (me_c + d % 2) % 2

    def node_from(d):
        return ((me_y - d // 2 + half) % half) * 2 + (me_c - d % 2 + 2) % 2

    def local_to(d):
        return (me_l + d) % locals_

    barrier = pltpu.get_barrier_semaphore()
    for d in range(nodes):
        for dl in range(locals_):
            if d or dl:
                pl.semaphore_signal(
                    barrier, inc=1, device_id={"node": node_to(d), "local": local_to(dl)},
                    device_id_type=MESH,
                )

    weight_copy = pltpu.make_async_copy(w_hbm.at[0], wv, w_sem)
    weight_copy.start()

    gates = gates_ref[...]
    weights = route_scale * gates / jnp.sum(gates, axis=0, keepdims=True)
    groups = jnp.concatenate(
        [groups_ref[j // share:j // share + 1, :] for j in range(picks)], axis=0
    )
    numbers = (picks_ref[...] * nodes + groups).astype(F32)
    lay = lax.broadcasted_iota(jnp.int32, (rows, pairs), 1) // picks == lax.broadcasted_iota(
        jnp.int32, (rows, pairs), 0
    )
    tables = jnp.dot(
        jnp.concatenate([weights, numbers], axis=0).astype(BF16),
        jnp.where(lay, 1.0, 0.0).astype(BF16),
        preferred_element_type=F32,
    )
    own = lax.broadcasted_iota(jnp.int32, (picks, pairs), 1) % picks == lax.broadcasted_iota(
        jnp.int32, (picks, pairs), 0
    )
    wts = jnp.sum(jnp.where(own, tables[:picks], 0.0), axis=0, keepdims=True)
    ids = jnp.sum(jnp.where(own, tables[picks:], 0.0), axis=0, keepdims=True).astype(jnp.int32)
    experts = nodes * locals_
    mine = lax.broadcasted_iota(jnp.int32, (experts, pairs), 0) == ids
    mine_f = jnp.where(mine, 1.0, 0.0)
    before = lax.broadcasted_iota(jnp.int32, (pairs, pairs), 0) < lax.broadcasted_iota(
        jnp.int32, (pairs, pairs), 1
    )
    running = jnp.dot(
        mine_f.astype(BF16), jnp.where(before, 1.0, 0.0).astype(BF16), preferred_element_type=F32
    )
    place = jnp.sum(mine_f * running, axis=0, keepdims=True).astype(jnp.int32)
    slot = ids * cap + place
    hot[...] = jnp.where(
        lax.broadcasted_iota(jnp.int32, (slots, pairs), 0) == slot, 1.0, 0.0
    ).astype(BF16)
    xs[...] = (
        jnp.dot(hot[...], hid_ref[...], preferred_element_type=F32).astype(BF16).reshape(xs.shape)
    )
    spread = jnp.where(lay, wts, 0.0).astype(BF16)
    mix_all = lax.dot_general(
        spread, hot[...], (((1,), (1,)), ((), ())), preferred_element_type=F32
    ).astype(BF16)
    span = nodes * cap
    for l in range(locals_):
        mix[l] = mix_all[:, l * span:(l + 1) * span]

    pl.semaphore_wait(barrier, nodes * locals_ - 1)

    order = list(range(nodes - 1, -1, -1))
    order = [d for d in order if d >= 2] + [d for d in order if d < 2]

    def hidden_copy(d, dl):
        n_t, l_t = node_to(d), local_to(dl)
        return pltpu.make_async_remote_copy(
            src_ref=xs.at[l_t * nodes + n_t], dst_ref=xr.at[d, me_l],
            send_sem=xsend.at[d, dl], recv_sem=xrecv.at[d, dl],
            device_id={"node": n_t, "local": l_t}, device_id_type=MESH,
        )

    def mix_copy(dl):
        l_t = local_to(dl)
        return pltpu.make_async_remote_copy(
            src_ref=mix.at[l_t], dst_ref=mixr.at[me_l],
            send_sem=asend.at[dl], recv_sem=arecv.at[dl],
            device_id={"node": me_n, "local": l_t}, device_id_type=MESH,
        )

    for k in range(0, nodes, 2):
        for dl in (2, 1, 3, 0):
            for d in order[k:k + 2]:
                if d or dl:
                    hidden_copy(d, dl).start()
    for dl in range(1, locals_):
        mix_copy(dl).start()
    xr[0, me_l] = xs[me_l * nodes + me_n]
    mixr[me_l] = mix[me_l]
    weight_copy.wait()

    def return_copy(c, d):
        return pltpu.make_async_remote_copy(
            src_ref=outb.at[c, d],
            dst_ref=zb.at[c, :, pl.ds(pl.multiple_of(me_n * cap, cap), cap), :],
            send_sem=zsend.at[c, d], recv_sem=zrecv.at[c, d],
            device_id={"node": node_from(d), "local": me_l}, device_id_type=MESH,
        )

    side = me_l // 2
    mate = me_l + 1 - 2 * (me_l % 2)
    inner = me_l == 1 + side
    edge = me_l != 1 + side
    away = (1 - side) * 2

    def mate_copy(c):
        return pltpu.make_async_remote_copy(
            src_ref=pb.at[c, mate], dst_ref=rb.at[c, 0],
            send_sem=psend.at[c, 0], recv_sem=precv.at[c, 0],
            device_id={"node": me_n, "local": mate}, device_id_type=MESH,
        )

    def forward_copy(c):
        return pltpu.make_async_remote_copy(
            src_ref=pb.at[c, pl.ds(away, 2)], dst_ref=mb.at[c],
            send_sem=psend.at[c, 1], recv_sem=precv.at[c, 1],
            device_id={"node": me_n, "local": mate}, device_id_type=MESH,
        )

    def cross_copy(c, t):
        return pltpu.make_async_remote_copy(
            src_ref=mb.at[c, t], dst_ref=rb.at[c, 1],
            send_sem=psend.at[c, 2 + t], recv_sem=precv.at[c, 2],
            device_id={"node": me_n, "local": away + t}, device_id_type=MESH,
        )

    lows = list(range(2, nodes, 2)) + [0]

    def hidden_wait(low):
        for d in (low, low + 1):
            for dl in range(locals_):
                if d or dl:
                    hidden_copy(d, dl).wait_recv()

    def apply(c, low):
        cols = pl.ds(pl.multiple_of(c * chunk, chunk), chunk)
        x = xr[low:low + 2].reshape(2 * locals_ * cap, xr.shape[-1])
        o = jnp.dot(x, wv[:, cols], preferred_element_type=F32).astype(BF16)
        o = o.reshape(2, locals_, cap, chunk)
        for k in range(2):
            if low + k:
                outb[c, low + k] = o[k]
                return_copy(c, low + k).start()
            else:
                zb[c, :, pl.ds(pl.multiple_of(me_n * cap, cap), cap), :] = o[k]

    ahead = min(5, chunks)
    for low in lows:
        hidden_wait(low)

        def early_chunk(c, carry, low=low):
            apply(c, low)
            return carry

        lax.fori_loop(0, ahead, early_chunk, 0)

    for dl in range(1, locals_):
        mix_copy(dl).wait_recv()

    def combine(c):
        for d in range(1, nodes):
            return_copy(c, d).wait_recv()
        for l in range(locals_):
            pb[c, l] = jnp.dot(mixr[l], zb[c, l], preferred_element_type=F32).astype(BF16)

        @pl.when(edge)
        def _():
            forward_copy(c).start()

        mate_copy(c).start()

    def merge(c):
        @pl.when(inner)
        def _():
            forward_copy(c).wait_recv()
            for t in range(2):
                mb[c, t] = (mb[c, t].astype(F32) + pb[c, away + t].astype(F32)).astype(BF16)
                cross_copy(c, t).start()

    def combine_chunk(c, carry):
        combine(c)

        @pl.when(c + ahead < chunks)
        def _():
            for low in lows:
                apply(c + ahead, low)

        @pl.when(c > 1)
        def _():
            merge(c - 2)

        return carry

    lax.fori_loop(0, chunks, combine_chunk, 0)
    merge(chunks - 2)
    merge(chunks - 1)

    def final_chunk(c, carry):
        cols = pl.ds(pl.multiple_of(c * chunk, chunk), chunk)
        mate_copy(c).wait_recv()
        cross_copy(c, 0).wait_recv()
        total = pb[c, me_l].astype(F32) + rb[c, 0].astype(F32) + rb[c, 1].astype(F32)
        out_ref[:, cols] = total.astype(BF16)
        return carry

    lax.fori_loop(0, chunks, final_chunk, 0)

    for d in range(nodes):
        for dl in range(locals_):
            if d or dl:
                hidden_copy(d, dl).wait_send()
    for dl in range(1, locals_):
        mix_copy(dl).wait_send()

    def drain(c, carry):
        for d in range(1, nodes):
            return_copy(c, d).wait_send()
        mate_copy(c).wait_send()

        @pl.when(edge)
        def _():
            forward_copy(c).wait_send()

        @pl.when(inner)
        def _():
            for t in range(2):
                cross_copy(c, t).wait_send()

        return carry

    lax.fori_loop(0, chunks, drain, 0)


def dense_plan(hidden, gates, node_groups, group_picks, down_weight, capacity):
    row_count, pick_count, hidden_width = hidden.shape
    nodes = lax.axis_size("node")
    locals_ = lax.axis_size("local")
    width = down_weight.shape[2]
    pairs = row_count * pick_count
    chunk = 256 if width % 256 == 0 else 128
    chunks = width // chunk
    dma = pltpu.SemaphoreType.DMA
    vmem = pl.BlockSpec(memory_space=pltpu.VMEM)
    return pl.pallas_call(
        functools.partial(fused_kernel, nodes, locals_, capacity, chunk),
        out_shape=jax.ShapeDtypeStruct((row_count, width), BF16),
        in_specs=[vmem, vmem, vmem, vmem, pl.BlockSpec(memory_space=pl.ANY)],
        out_specs=vmem,
        scratch_shapes=[
            pltpu.VMEM((nodes * locals_ * capacity, pairs), BF16),
            pltpu.VMEM((nodes * locals_, capacity, hidden_width), BF16),
            pltpu.VMEM((nodes, locals_, capacity, hidden_width), BF16),
            pltpu.VMEM((locals_, row_count, nodes * capacity), BF16),
            pltpu.VMEM((locals_, row_count, nodes * capacity), BF16),
            pltpu.VMEM((hidden_width, width), BF16),
            pltpu.VMEM((chunks, nodes, locals_, capacity, chunk), BF16),
            pltpu.VMEM((chunks, locals_, nodes * capacity, chunk), BF16),
            pltpu.VMEM((chunks, locals_, row_count, chunk), BF16),
            pltpu.VMEM((chunks, 2, row_count, chunk), BF16),
            pltpu.VMEM((chunks, 2, row_count, chunk), BF16),
            dma,
            dma((nodes, locals_)),
            dma((nodes, locals_)),
            dma((locals_,)),
            dma((locals_,)),
            dma((chunks, nodes)),
            dma((chunks, nodes)),
            dma((chunks, 4)),
            dma((chunks, 3)),
        ],
        compiler_params=pltpu.CompilerParams(
            collective_id=0, has_side_effects=True, vmem_limit_bytes=56 * 1024 * 1024
        ),
    )(
        gates.T,
        node_groups.T,
        group_picks.T,
        hidden.reshape(pairs, hidden_width),
        down_weight,
    )


def shards(hidden, gates, node_groups, group_picks, down_weight):
    row_count = hidden.shape[0]
    nodes = lax.axis_size("node")
    capacity = 2 * row_count // lax.axis_size("local")
    if nodes == node_groups.shape[1] and nodes % 2 == 0 and lax.axis_size("local") == 4:
        return dense_plan(hidden, gates, node_groups, group_picks, down_weight, capacity)
    route_weights = (route_scale * gates / jnp.sum(gates, axis=1, keepdims=True)).astype(BF16)
    return sparse_plan(
        hidden, route_weights, node_groups, group_picks, down_weight[0], capacity
    )


def solution(mesh):
    return jax.shard_map(
        shards,
        mesh=mesh,
        in_specs=(
            P(("groups", "node", "local"), None, None),
            P(("groups", "node", "local"), None),
            P(("groups", "node", "local"), None),
            P(("groups", "node", "local"), None),
            P(("node", "local"), None, None),
        ),
        out_specs=P(("groups", "node", "local"), None),
        check_vma=False,
    )
```
